32 devices in a mesh: slab: 2 (over y), ma: 4 (over z), freq: 2 (over x), pol: 2 (over core).
Axes of the slice: x: 2, y: 2, z: 4, core: 2. Of those that a mesh axis runs over, the one named last changes fastest.
Arguments:
- visibility: bfloat16 [16, 2, 64, 8192], P(('slab', 'freq'), None, 'pol', 'ma'), parts along dimension 0, may hold values from -6 to 6
- beam_rows: bfloat16 [16, 64, 768], P(('slab', 'freq'), 'pol'), parts along dimension 0, may hold values from -0.4375 to 0.4375
- mode_gain: float32 [192, 768], P('ma'), may hold values from 0.7 to 1.5
- harmonic_basis: bfloat16 [768, 768], replicated, may hold values from -0.21875 to 0.21875
- step_size: float32 [16], P(('slab', 'freq')), parts along dimension 0, may hold values from 0.15 to 0.25
- kl_matrix: bfloat16 [4, 8], P('slab'), parts along dimension 0, may hold values from -2 to 2
Outputs:
- filtered: bfloat16 [192, 4, 2, 768], P('ma', ('slab', 'freq'), 'pol'), parts along dimension 1
The draws below stay inside these ranges and needn't reach their ends.
There are 2 independent parts, one for each index of `slab`. The reference program is written for one: setup_inputs(seed, part) draws one part's arguments, and reference() takes and returns one part's arrays. A program takes and returns all parts, laid end to end along the dimension named above; an argument that names none is the same for every part. Nothing has to cross between parts.
All inputs are finite; a program needn't handle non-finite values.
Results may differ from the reference program's by a relative error of at most 0.0088.
Values may be sent and summed in bfloat16 or wider, within the bound.
A program may use at most 64 MiB of HBM per device.

```python
import math
import jax
import jax.numpy as jnp

NT = 8192
L = 768
M = 192
FREQS = 8
KEEP = 2
BASE = 64
ITERS = 2


def levels(key, extent, cuts, low, largest):
    level, own = 1.0, jax.random.fold_in(key, 6)
    for dim, parts in cuts:
        steps = jnp.exp(jax.random.uniform(jax.random.fold_in(own, dim), (parts,), jnp.float32, low / len(cuts), largest / len(cuts)))
        level = level * jnp.repeat(steps, extent[dim] // parts).reshape([-1 if axis == dim else 1 for axis in range(len(extent))])
    return level


def gaussian(rng, shape, spread, most, shards=(), kind=jnp.bfloat16):
    values = jax.random.normal(rng, shape, jnp.float32) * spread
    if len(shards) > 0:
        values = levels(rng, shape, shards, -0.22, 0.18) * values
    return jnp.clip(values, min=-most, max=most).astype(kind)


def setup_inputs(seed: int = 0, part: int = 0) -> dict:
    keys = jax.random.split(jax.random.key(seed), 7)
    part_keys = jax.random.split(jax.random.fold_in(keys[6], part), 7)
    return {
        "visibility": gaussian(part_keys[0], (FREQS, 2, BASE, NT), 1.0, 6.0, ((0, 2), (2, 2), (3, 4))),
        "beam_rows": gaussian(part_keys[1], (FREQS, BASE, L), (L // 4) ** -0.5, 0.4375, ((0, 2), (1, 2))),
        "mode_gain": jnp.clip(jnp.exp(math.log(1.5) - 0.7621401 * jax.random.uniform(keys[2], (M, L), jnp.float32) ** levels(keys[2], (M, L), ((0, 4),), -0.2, 0.2)), 0.7, 1.5),
        "harmonic_basis": gaussian(keys[3], (L, L), L ** -0.5, 0.21875),
        "step_size": jnp.clip(0.15 + 0.099999994 * jax.random.uniform(part_keys[4], (FREQS,), jnp.float32) ** levels(part_keys[4], (FREQS,), ((0, 2),), -0.2, 0.2), 0.15, 0.25),
        "kl_matrix": gaussian(part_keys[5], (KEEP, FREQS), FREQS ** -0.5, 2.0),
    }


def spectral_tables(time_index, mode_index, total):
    phase = (time_index[:, None] * mode_index[None, :]) % total
    angle = phase.astype(jnp.float32) * (2.0 * jnp.pi / total)
    return jnp.cos(angle).astype(jnp.bfloat16), jnp.sin(angle).astype(jnp.bfloat16)


def reference(visibility, beam_rows, mode_gain, harmonic_basis, step_size, kl_matrix):
    nfreq = visibility.shape[0]
    nbase = visibility.shape[2]
    cosine, sine = spectral_tables(jnp.arange(NT, dtype=jnp.int32), jnp.arange(M, dtype=jnp.int32), NT)
    flat = visibility.reshape(nfreq * 2 * nbase, NT)
    first = jnp.dot(flat, cosine, preferred_element_type=jnp.float32).reshape(nfreq, 2, nbase, M)
    second = jnp.dot(flat, sine, preferred_element_type=jnp.float32).reshape(nfreq, 2, nbase, M)
    spectrum = jnp.stack([first[:, 0] + second[:, 1], first[:, 1] - second[:, 0]], axis=1) * (NT ** -0.5)
    modes = spectrum.transpose(3, 0, 1, 2).astype(jnp.bfloat16)
    mask = (jnp.arange(L)[None, :] >= jnp.arange(M)[:, None]).astype(jnp.float32)
    beam = beam_rows.astype(jnp.float32)

    def back(signal):
        summed = jnp.einsum('mfpb,fbk->mfpk', signal.astype(jnp.float32), beam)
        scaled = (summed * mode_gain[:, None, None, :]).astype(jnp.bfloat16)
        result = jnp.dot(scaled.reshape(-1, L), harmonic_basis, preferred_element_type=jnp.float32)
        return result.reshape(scaled.shape) * mask[:, None, None, :]

    def fore(coeffs):
        sampled = jnp.einsum('mfpl,kl->mfpk', coeffs.astype(jnp.float32), harmonic_basis.astype(jnp.float32))
        scaled = (sampled * mode_gain[:, None, None, :]).astype(jnp.bfloat16)
        return jnp.einsum('mfpk,fbk->mfpb', scaled.astype(jnp.float32), beam).astype(jnp.bfloat16)

    dirty = back(modes)
    stepping = step_size[None, :, None, None]
    estimate = stepping * dirty
    for counter in range(ITERS):
        rounded = estimate.astype(jnp.bfloat16)
        estimate = estimate + stepping * (dirty - back(fore(rounded)))
    rounded = estimate.astype(jnp.bfloat16)
    result = jnp.einsum('jf,mfpl->mjpl', kl_matrix.astype(jnp.float32), rounded.astype(jnp.float32))
    return result.astype(jnp.bfloat16)
```

```python
import functools

import jax
import jax.numpy as jnp
import ml_dtypes
import numpy as np
from jax import lax
from jax.experimental import pallas as pl
from jax.experimental.pallas import tpu as pltpu
from jax.sharding import PartitionSpec as P

ITERS = 2
MESH = pl.DeviceIdType.MESH
NT_DIMS = (((1,), (1,)), ((), ()))


def spectral_tables(modes, local_time, total):
    phase = np.outer(np.arange(modes), np.arange(local_time)) % total
    angle = phase * (2.0 * np.pi / total)
    both = np.concatenate([np.cos(angle), np.sin(angle)], axis=0)
    return both.astype(np.float32).astype(ml_dtypes.bfloat16)


def dot(left, right):
    return jnp.dot(left, right, preferred_element_type=jnp.float32)


def dot_t(left, right):
    return lax.dot_general(left, right, NT_DIMS, preferred_element_type=jnp.float32)


def kernel(
    sizes,
    vis_hbm,
    table_hbm,
    beam_hbm,
    gain_hbm,
    basis_hbm,
    step_ref,
    kl_ref,
    out_ref,
    vis_v,
    table_v,
    beam_v,
    gain_v,
    basis_v,
    dirty_v,
    est_v,
    send_v,
    recv_v,
    klsend_v,
    klrecv_v,
    load_sem,
    send_sem,
    recv_sem,
    beam_sem,
    klsend_sem,
    klrecv_sem,
):
    n_ma, n_pol, n_freq = sizes
    a, p, fr = lax.axis_index("ma"), lax.axis_index("pol"), lax.axis_index("freq")
    _, nfreq, nbase, ntime = vis_v.shape
    local_modes, degrees = gain_v.shape
    all_modes = local_modes * n_ma
    half = nfreq * nbase
    peers = [(da, dp) for da in range(n_ma) for dp in range(n_pol) if (da, dp) != (0, 0)]
    peers.sort(key=lambda o: (abs(o[0] - n_ma // 2), o[1]))

    tchunks = table_v.shape[0]
    tsize = ntime // tchunks
    spectral = []
    for i in range(tchunks):
        cols = pl.ds(i * tsize, tsize)
        group = [
            pltpu.make_async_copy(
                vis_hbm.at[:, part, :, cols], vis_v.at[part, :, :, cols], load_sem.at[3 * i + part]
            )
            for part in range(2)
        ]
        group.append(pltpu.make_async_copy(table_hbm.at[i], table_v.at[i], load_sem.at[3 * i + 2]))
        for c in group:
            c.start()
        spectral.append(group)
    base = 3 * tchunks
    load_beam = pltpu.make_async_copy(beam_hbm, beam_v.at[p], load_sem.at[base])
    load_gain = pltpu.make_async_copy(gain_hbm, gain_v, load_sem.at[base + 1])
    load_basis = pltpu.make_async_copy(basis_hbm, basis_v, load_sem.at[base + 2])
    for c in (load_beam, load_gain, load_basis):
        c.start()

    barrier = pltpu.get_barrier_semaphore()

    def group_id(da, dp):
        return {"ma": lax.rem(a + da, n_ma), "pol": lax.rem(p + dp, n_pol)}

    def freq_id(df):
        return {"freq": lax.rem(fr + df, n_freq)}

    for da, dp in peers:
        pl.semaphore_signal(barrier, inc=1, device_id=group_id(da, dp), device_id_type=MESH)
    for df in range(1, n_freq):
        pl.semaphore_signal(barrier, inc=1, device_id=freq_id(df), device_id_type=MESH)

    total = None
    for i in range(tchunks):
        for c in spectral[i]:
            c.wait()
        samples = vis_v[:, :, :, i * tsize : (i + 1) * tsize].reshape(2 * half, tsize)
        term = dot_t(table_v[i], samples)
        total = term if total is None else total + term
    cosine, sine = total[:all_modes], total[all_modes:]
    real = cosine[:, :half] + sine[:, half:]
    imag = cosine[:, half:] - sine[:, :half]
    turn = lax.rem(a * lax.broadcasted_iota(jnp.int32, (all_modes, half), 0), n_ma)
    scale = float(ntime * n_ma) ** -0.5
    pc = jnp.full((all_modes, half), scale, jnp.float32)
    ps = jnp.zeros((all_modes, half), jnp.float32)
    for r in range(1, n_ma):
        angle = 2.0 * np.pi * r / n_ma
        pc = jnp.where(turn == r, float(scale * np.cos(angle)), pc)
        ps = jnp.where(turn == r, float(scale * np.sin(angle)), ps)
    block = (n_ma, local_modes, half)
    send_v[0] = (real * pc + imag * ps).astype(jnp.bfloat16).reshape(block)
    send_v[1] = (imag * pc - real * ps).astype(jnp.bfloat16).reshape(block)

    pl.semaphore_wait(barrier, len(peers) + n_freq - 1)
    copies = []
    for i, (da, dp) in enumerate(peers):
        to = group_id(da, dp)
        copy = pltpu.make_async_remote_copy(
            src_ref=send_v.at[to["pol"], to["ma"]],
            dst_ref=recv_v.at[p, a],
            send_sem=send_sem.at[i],
            recv_sem=recv_sem.at[i],
            device_id=to,
            device_id_type=MESH,
        )
        copy.start()
        copies.append(copy)
    beam_copies = []
    for dp in range(1, n_pol):
        copy = pltpu.make_async_remote_copy(
            src_ref=beam_hbm,
            dst_ref=beam_v.at[p],
            send_sem=beam_sem.at[0, dp - 1],
            recv_sem=beam_sem.at[1, dp - 1],
            device_id={"pol": lax.rem(p + dp, n_pol)},
            device_id_type=MESH,
        )
        copy.start()
        beam_copies.append(copy)
    recv_v[p, a] = send_v[p, a]

    kl = kl_ref[...].astype(jnp.float32)
    kl_row = lax.broadcasted_iota(jnp.int32, kl.shape, 0)
    kl_col = lax.broadcasted_iota(jnp.int32, kl.shape, 1)
    kept = kl.shape[0] // n_freq
    weights = []
    for df in range(n_freq):
        first = lax.rem(fr + df, n_freq) * kept
        weights.append(
            [
                [
                    jnp.sum(
                        jnp.where((kl_row == first + j) & (kl_col == fr * nfreq + f), kl, 0.0),
                        axis=(0, 1),
                        keepdims=True,
                    )
                    for f in range(nfreq)
                ]
                for j in range(kept)
            ]
        )
    for c in (load_beam, load_gain, load_basis):
        c.wait()
    lane = lax.rem(lax.broadcasted_iota(jnp.int32, (local_modes, n_pol * half), 1), half)
    own = [(lane >= f * nbase) & (lane < (f + 1) * nbase) for f in range(nfreq)]
    mode = lax.broadcasted_iota(jnp.int32, (local_modes, degrees), 0) + a * local_modes
    keep = lax.broadcasted_iota(jnp.int32, (local_modes, degrees), 1) >= mode

    for copy in beam_copies:
        copy.wait_recv()
    for copy in copies:
        copy.wait_recv()

    def spread(blocks):
        return jnp.concatenate(
            [jnp.where(own[f], blocks[f], 0.0) for f in range(nfreq)], axis=0
        ).astype(jnp.bfloat16)

    def with_gain(value):
        value = value.reshape(nfreq, local_modes, degrees) * gain_v[...][None]
        return value.astype(jnp.bfloat16).reshape(nfreq * local_modes, degrees)

    def rows():
        return beam_v[...].reshape(n_pol * half, degrees)

    def fore(x):
        q = with_gain(dot_t(x, basis_v[...]))
        y = dot_t(q, rows())
        return spread([y[f * local_modes : (f + 1) * local_modes] for f in range(nfreq)])

    halves = []
    for q in range(n_pol):
        summed = recv_v[q, 0].astype(jnp.float32)
        for s in range(1, n_ma):
            summed = summed + recv_v[q, s].astype(jnp.float32)
        halves.append(summed)
    signal = spread([jnp.concatenate(halves, axis=1)] * nfreq)

    dirty = dot(with_gain(dot(signal, rows())), basis_v[...])
    for f in range(nfreq):
        value = jnp.where(keep, dirty[f * local_modes : (f + 1) * local_modes], 0.0)
        dirty_v[f] = value
        est_v[f] = value * step_ref[f]

    def rounded():
        return est_v[...].astype(jnp.bfloat16).reshape(nfreq * local_modes, degrees)

    for _ in range(ITERS - 1):
        again = dot(with_gain(dot(fore(rounded()), rows())), basis_v[...])
        for f in range(nfreq):
            value = jnp.where(keep, again[f * local_modes : (f + 1) * local_modes], 0.0)
            est_v[f] = est_v[f] + step_ref[f] * (dirty_v[f] - value)

    h = with_gain(dot(fore(rounded()), rows()))
    chunks = klsend_v.shape[1]
    width = degrees // chunks
    kl_copies = []
    held = []
    for i in range(chunks):
        cols = slice(i * width, (i + 1) * width)
        again = dot(h, basis_v[:, cols])
        final = []
        for f in range(nfreq):
            value = jnp.where(keep[:, cols], again[f * local_modes : (f + 1) * local_modes], 0.0)
            value = est_v[f, :, cols] + step_ref[f] * (dirty_v[f, :, cols] - value)
            final.append(value.astype(jnp.bfloat16).astype(jnp.float32))
        group = []
        for df in [*range(1, n_freq), 0]:
            terms = []
            for j in range(kept):
                term = weights[df][j][0] * final[0]
                for f in range(1, nfreq):
                    term = term + weights[df][j][f] * final[f]
                terms.append(term)
            if df == 0:
                held.append(terms)
                continue
            for j in range(kept):
                klsend_v[df - 1, i, j] = terms[j].astype(jnp.bfloat16)
            copy = pltpu.make_async_remote_copy(
                src_ref=klsend_v.at[df - 1, i],
                dst_ref=klrecv_v.at[df - 1, i],
                send_sem=klsend_sem.at[df - 1, i],
                recv_sem=klrecv_sem.at[df - 1, i],
                device_id=freq_id(df),
                device_id_type=MESH,
            )
            copy.start()
            group.append(copy)
        kl_copies.append(group)

    for copy in copies:
        copy.wait_send()
    for copy in beam_copies:
        copy.wait_send()
    for i in range(chunks):
        for df, copy in enumerate(kl_copies[i], 1):
            copy.wait_recv()
            for j in range(kept):
                held[i][j] = held[i][j] + klrecv_v[df - 1, i, j].astype(jnp.float32)
        for j in range(kept):
            out_ref[j, :, i * width : (i + 1) * width] = held[i][j].astype(jnp.bfloat16)
    for group in kl_copies:
        for copy in group:
            copy.wait_send()


def on_device(sizes, visibility, beam_rows, mode_gain, harmonic_basis, step_size, kl_matrix):
    n_ma, n_pol, n_freq = sizes
    nfreq, _, nbase, ntime = visibility.shape
    local_modes, degrees = mode_gain.shape
    kept = kl_matrix.shape[0] // n_freq
    half = nfreq * nbase
    all_modes = local_modes * n_ma
    tchunks = 2 if ntime % 512 == 0 else 1
    chunks = 3 if degrees % 384 == 0 else 1
    table = spectral_tables(all_modes, ntime, ntime * n_ma)
    table = np.ascontiguousarray(table.reshape(2 * all_modes, tchunks, -1).transpose(1, 0, 2))
    peers = n_ma * n_pol - 1
    hops = max(n_freq - 1, 1)
    dma = pltpu.SemaphoreType.DMA
    kl_shape = (hops, chunks, kept, local_modes, degrees // chunks)
    out = pl.pallas_call(
        functools.partial(kernel, sizes),
        out_shape=jax.ShapeDtypeStruct((kept, local_modes, degrees), jnp.bfloat16),
        in_specs=[pl.BlockSpec(memory_space=pl.ANY)] * 5
        + [pl.BlockSpec(memory_space=pltpu.SMEM), pl.BlockSpec(memory_space=pltpu.VMEM)],
        out_specs=pl.BlockSpec(memory_space=pltpu.VMEM),
        scratch_shapes=[
            pltpu.VMEM((2, nfreq, nbase, ntime), jnp.bfloat16),
            pltpu.VMEM(table.shape, jnp.bfloat16),
            pltpu.VMEM((n_pol, nfreq, nbase, degrees), jnp.bfloat16),
            pltpu.VMEM((local_modes, degrees), jnp.float32),
            pltpu.VMEM(harmonic_basis.shape, jnp.bfloat16),
            pltpu.VMEM((nfreq, local_modes, degrees), jnp.float32),
            pltpu.VMEM((nfreq, local_modes, degrees), jnp.float32),
            pltpu.VMEM((2, n_ma, local_modes, half), jnp.bfloat16),
            pltpu.VMEM((n_pol, n_ma, local_modes, half), jnp.bfloat16),
            pltpu.VMEM(kl_shape, jnp.bfloat16),
            pltpu.VMEM(kl_shape, jnp.bfloat16),
            dma((3 * tchunks + 3,)),
            dma((peers,)),
            dma((peers,)),
            dma((2, max(n_pol - 1, 1))),
            dma((hops, chunks)),
            dma((hops, chunks)),
        ],
        compiler_params=pltpu.CompilerParams(
            collective_id=0, has_side_effects=True, vmem_limit_bytes=56 * 2**20
        ),
    )(
        visibility,
        jnp.asarray(table),
        beam_rows,
        mode_gain,
        harmonic_basis,
        step_size,
        kl_matrix,
    )
    return out.transpose(1, 0, 2)[:, :, None, :]


def solution(mesh):
    sizes = (mesh.shape["ma"], mesh.shape["pol"], mesh.shape["freq"])
    placed = (
        P(("slab", "freq"), None, "pol", "ma"),
        P(("slab", "freq"), "pol", None),
        P("ma", None),
        P(),
        P(("slab", "freq")),
        P("slab", None),
    )
    return jax.shard_map(
        functools.partial(on_device, sizes),
        mesh=mesh,
        in_specs=placed,
        out_specs=P("ma", ("slab", "freq"), "pol", None),
        check_vma=False,
    )
```

```python
import functools

import jax
import jax.numpy as jnp
import ml_dtypes
import numpy as np
from jax import lax
from jax.experimental import pallas as pl
from jax.experimental.pallas import tpu as pltpu
from jax.sharding import PartitionSpec as P

ITERS = 2
MESH = pl.DeviceIdType.MESH
NT_DIMS = (((1,), (1,)), ((), ()))


def spectral_tables(modes, local_time, total):
    phase = np.outer(np.arange(modes), np.arange(local_time)) % total
    angle = phase * (2.0 * np.pi / total)
    both = np.concatenate([np.cos(angle), np.sin(angle)], axis=0)
    return both.astype(np.float32).astype(ml_dtypes.bfloat16)


def dot(left, right):
    return jnp.dot(left, right, preferred_element_type=jnp.float32)


def dot_t(left, right):
    return lax.dot_general(left, right, NT_DIMS, preferred_element_type=jnp.float32)


def kernel(
    sizes,
    vis_hbm,
    table_hbm,
    beam_hbm,
    gain_hbm,
    basis_hbm,
    step_hbm,
    kl_hbm,
    out_ref,
    vis_v,
    table_v,
    beam_v,
    gain_v,
    basis_v,
    step_s,
    kl_v,
    send_v,
    recv_v,
    ysend_v,
    yrecv_v,
    load_sem,
    send_sem,
    recv_sem,
    pol_sem,
    freq_sem,
    pass_sem,
    y_sem,
):
    n_ma, n_pol, n_freq = sizes
    a, p, fr = lax.axis_index("ma"), lax.axis_index("pol"), lax.axis_index("freq")
    _, nfreq, nbase, ntime = vis_v.shape
    local_modes, degrees = gain_v.shape
    all_modes = local_modes * n_ma
    half = nfreq * nbase
    full = n_pol * half
    kept = kl_v.shape[0] // n_freq
    peers = [(da, dp) for da in range(n_ma) for dp in range(n_pol) if (da, dp) != (0, 0)]
    peers.sort(key=lambda o: (abs(o[0] - n_ma // 2), o[1]))

    tchunks = table_v.shape[0]
    tsize = ntime // tchunks
    spectral = []
    for i in range(tchunks):
        cols = pl.ds(i * tsize, tsize)
        group = [
            pltpu.make_async_copy(
                vis_hbm.at[:, part, :, cols], vis_v.at[part, :, :, cols], load_sem.at[3 * i + part]
            )
            for part in range(2)
        ]
        group.append(pltpu.make_async_copy(table_hbm.at[i], table_v.at[i], load_sem.at[3 * i + 2]))
        for c in group:
            c.start()
        spectral.append(group)
    loads = [
        pltpu.make_async_copy(src, dst, load_sem.at[3 * tchunks + i])
        for i, (src, dst) in enumerate(
            [
                (step_hbm, step_s),
                (kl_hbm, kl_v),
                (basis_hbm, basis_v),
                (beam_hbm, beam_v.at[fr, p]),
                (gain_hbm, gain_v),
            ]
        )
    ]
    for c in loads:
        c.start()

    barrier = pltpu.get_barrier_semaphore()

    def group_id(da, dp):
        return {"ma": lax.rem(a + da, n_ma), "pol": lax.rem(p + dp, n_pol)}

    def freq_id(df):
        return {"freq": lax.rem(fr + df, n_freq)}

    def remote(src, dst, send, recv, to):
        copy = pltpu.make_async_remote_copy(
            src_ref=src,
            dst_ref=dst,
            send_sem=send,
            recv_sem=recv,
            device_id=to,
            device_id_type=MESH,
        )
        copy.start()
        return copy

    for da, dp in peers:
        pl.semaphore_signal(barrier, inc=1, device_id=group_id(da, dp), device_id_type=MESH)
    for df in range(1, n_freq):
        pl.semaphore_signal(barrier, inc=1, device_id=freq_id(df), device_id_type=MESH)

    total = None
    for i in range(tchunks):
        for c in spectral[i]:
            c.wait()
        samples = vis_v[:, :, :, i * tsize : (i + 1) * tsize].reshape(2 * half, tsize)
        term = dot_t(table_v[i], samples)
        total = term if total is None else total + term
    cosine, sine = total[:all_modes], total[all_modes:]
    real = cosine[:, :half] + sine[:, half:]
    imag = cosine[:, half:] - sine[:, :half]
    turn = lax.rem(a * lax.broadcasted_iota(jnp.int32, (all_modes, half), 0), n_ma)
    scale = float(ntime * n_ma) ** -0.5
    pc = jnp.full((all_modes, half), scale, jnp.float32)
    ps = jnp.zeros((all_modes, half), jnp.float32)
    for r in range(1, n_ma):
        angle = 2.0 * np.pi * r / n_ma
        pc = jnp.where(turn == r, float(scale * np.cos(angle)), pc)
        ps = jnp.where(turn == r, float(scale * np.sin(angle)), ps)
    block = (n_ma, local_modes, half)
    send_v[0] = (real * pc + imag * ps).astype(jnp.bfloat16).reshape(block)
    send_v[1] = (imag * pc - real * ps).astype(jnp.bfloat16).reshape(block)

    pl.semaphore_wait(barrier, len(peers) + n_freq - 1)
    copies = []
    for i, (da, dp) in enumerate(peers):
        to = group_id(da, dp)
        src = send_v.at[to["pol"], to["ma"]]
        copies.append(remote(src, recv_v.at[p, a], send_sem.at[i], recv_sem.at[i], to))
    mine = beam_v.at[fr, p]
    pol_copies = [
        remote(beam_hbm, mine, pol_sem.at[0, d - 1], pol_sem.at[1, d - 1], group_id(0, d))
        for d in range(1, n_pol)
    ]
    freq_copies = [
        remote(beam_hbm, mine, freq_sem.at[0, d - 1], freq_sem.at[1, d - 1], freq_id(d))
        for d in range(1, n_freq)
    ]
    recv_v[p, a] = send_v[p, a]

    for c in loads:
        c.wait()
    lane = lax.rem(lax.broadcasted_iota(jnp.int32, (local_modes, full), 1), half)
    own = [(lane >= f * nbase) & (lane < (f + 1) * nbase) for f in range(nfreq)]
    mode = lax.broadcasted_iota(jnp.int32, (local_modes, degrees), 0) + a * local_modes
    keep = lax.broadcasted_iota(jnp.int32, (local_modes, degrees), 1) >= mode
    kl = kl_v[...].astype(jnp.float32)
    kl_row = lax.broadcasted_iota(jnp.int32, kl.shape, 0)
    kl_col = lax.broadcasted_iota(jnp.int32, kl.shape, 1)

    def kl_weight(j, f):
        chosen = (kl_row == j) & (kl_col == fr * nfreq + f)
        return jnp.sum(jnp.where(chosen, kl, 0.0), axis=(0, 1), keepdims=True)

    def lane_weights(df):
        weights = []
        for j in range(kept):
            row = jnp.zeros((1, full), jnp.float32)
            for f in range(nfreq):
                value = kl_weight(lax.rem(fr + df, n_freq) * kept + j, f)
                row = jnp.where(own[f][:1], value, row)
            weights.append(row)
        return weights

    weights = [lane_weights(df) for df in range(n_freq)]
    steps = jnp.zeros((1, full), jnp.float32)
    for f in range(nfreq):
        steps = jnp.where(own[f][:1], step_s[f], steps)

    for copy in pol_copies + copies:
        copy.wait_recv()

    def spread(value):
        return jnp.concatenate(
            [jnp.where(own[f], value, 0.0) for f in range(nfreq)], axis=0
        ).astype(jnp.bfloat16)

    def gather(value):
        result = jnp.zeros((local_modes, full), jnp.float32)
        for f in range(nfreq):
            result = jnp.where(own[f], value[f * local_modes : (f + 1) * local_modes], result)
        return result

    def with_gain(value):
        value = value.reshape(-1, local_modes, degrees) * gain_v[...][None]
        return value.astype(jnp.bfloat16).reshape(-1, degrees)

    def masked(value):
        value = value.reshape(-1, local_modes, degrees)
        return jnp.where(keep[None], value, 0.0).astype(jnp.bfloat16).reshape(-1, degrees)

    def again(y):
        rows = beam_v[fr].reshape(full, degrees)
        coeffs = masked(dot(with_gain(dot(spread(y), rows)), basis_v[...]))
        return gather(dot_t(with_gain(dot_t(coeffs, basis_v[...])), rows))

    halves = []
    for q in range(n_pol):
        summed = recv_v[q, 0].astype(jnp.float32)
        for s in range(1, n_ma):
            summed = summed + recv_v[q, s].astype(jnp.float32)
        halves.append(summed)
    z = steps * jnp.concatenate(halves, axis=1)
    y = z
    pass_copies = []
    for it in range(ITERS):
        y = y + z - steps * again(y)
        if it == 0:
            for d, copy in enumerate(freq_copies, 1):
                copy.wait_recv()
                slot = beam_v.at[lax.rem(fr + n_freq - d, n_freq), p]
                for dp in range(1, n_pol):
                    sems = (pass_sem.at[0, d - 1, dp - 1], pass_sem.at[1, d - 1, dp - 1])
                    pass_copies.append(remote(slot, slot, *sems, group_id(0, dp)))

    y_copies = []
    for d in range(1, n_freq):
        for j in range(kept):
            ysend_v[d - 1, j] = (y * weights[d][j]).astype(jnp.bfloat16)
        sems = (y_sem.at[0, d - 1], y_sem.at[1, d - 1])
        y_copies.append(remote(ysend_v.at[d - 1], yrecv_v.at[fr], *sems, freq_id(d)))
    for j in range(kept):
        yrecv_v[fr, j] = (y * weights[0][j]).astype(jnp.bfloat16)

    for copy in pass_copies + y_copies:
        copy.wait_recv()
    left = jnp.concatenate(
        [yrecv_v[s].reshape(kept * local_modes, full) for s in range(n_freq)], axis=1
    )
    g = dot(left, beam_v[...].reshape(n_freq * full, degrees))
    out_ref[...] = masked(dot(with_gain(g), basis_v[...])).reshape(out_ref.shape)
    for copy in copies + pol_copies + freq_copies + pass_copies + y_copies:
        copy.wait_send()


def store_kernel(src, dst, sem):
    copy = pltpu.make_async_copy(src, dst, sem)
    copy.start()
    copy.wait()


def on_device(sizes, visibility, beam_rows, mode_gain, harmonic_basis, step_size, kl_matrix):
    n_ma, n_pol, n_freq = sizes
    nfreq, _, nbase, ntime = visibility.shape
    local_modes, degrees = mode_gain.shape
    kept = kl_matrix.shape[0] // n_freq
    half = nfreq * nbase
    full = n_pol * half
    all_modes = local_modes * n_ma
    tchunks = 2 if ntime % 512 == 0 else 1
    table = spectral_tables(all_modes, ntime, ntime * n_ma)
    table = np.ascontiguousarray(table.reshape(2 * all_modes, tchunks, -1).transpose(1, 0, 2))
    peers = n_ma * n_pol - 1
    hops, cores = max(n_freq - 1, 1), max(n_pol - 1, 1)
    dma = pltpu.SemaphoreType.DMA
    out_shape = (kept, local_modes, degrees)
    out = pl.pallas_call(
        functools.partial(kernel, sizes),
        out_shape=pltpu.VMEM(out_shape, jnp.bfloat16),
        in_specs=[pl.BlockSpec(memory_space=pl.ANY)] * 7,
        out_specs=pl.BlockSpec(memory_space=pltpu.VMEM),
        scratch_shapes=[
            pltpu.VMEM((2, nfreq, nbase, ntime), jnp.bfloat16),
            pltpu.VMEM(table.shape, jnp.bfloat16),
            pltpu.VMEM((n_freq, n_pol, nfreq, nbase, degrees), jnp.bfloat16),
            pltpu.VMEM((local_modes, degrees), jnp.float32),
            pltpu.VMEM(harmonic_basis.shape, jnp.bfloat16),
            pltpu.SMEM(step_size.shape, jnp.float32),
            pltpu.VMEM(kl_matrix.shape, jnp.bfloat16),
            pltpu.VMEM((2, n_ma, local_modes, half), jnp.bfloat16),
            pltpu.VMEM((n_pol, n_ma, local_modes, half), jnp.bfloat16),
            pltpu.VMEM((hops, kept, local_modes, full), jnp.bfloat16),
            pltpu.VMEM((n_freq, kept, local_modes, full), jnp.bfloat16),
            dma((3 * tchunks + 5,)),
            dma((peers,)),
            dma((peers,)),
            dma((2, cores)),
            dma((2, hops)),
            dma((2, hops, cores)),
            dma((2, hops)),
        ],
        compiler_params=pltpu.CompilerParams(
            collective_id=0, has_side_effects=True, vmem_limit_bytes=56 * 2**20
        ),
    )(
        visibility,
        jnp.asarray(table),
        beam_rows,
        mode_gain,
        harmonic_basis,
        step_size,
        kl_matrix,
    )
    out = pl.pallas_call(
        store_kernel,
        out_shape=jax.ShapeDtypeStruct(out_shape, jnp.bfloat16),
        in_specs=[pl.BlockSpec(memory_space=pl.ANY)],
        out_specs=pl.BlockSpec(memory_space=pl.ANY),
        scratch_shapes=[dma],
    )(out)
    return out.transpose(1, 0, 2)[:, :, None, :]


def solution(mesh):
    sizes = (mesh.shape["ma"], mesh.shape["pol"], mesh.shape["freq"])
    placed = (
        P(("slab", "freq"), None, "pol", "ma"),
        P(("slab", "freq"), "pol", None),
        P("ma", None),
        P(),
        P(("slab", "freq")),
        P("slab", None),
    )
    return jax.shard_map(
        functools.partial(on_device, sizes),
        mesh=mesh,
        in_specs=placed,
        out_specs=P("ma", ("slab", "freq"), "pol", None),
        check_vma=False,
    )
```

```python
import functools

import jax
import jax.numpy as jnp
import ml_dtypes
import numpy as np
from jax import lax
from jax.experimental import pallas as pl
from jax.experimental.pallas import tpu as pltpu
from jax.sharding import PartitionSpec as P

ITERS = 2
MESH = pl.DeviceIdType.MESH
NT_DIMS = (((1,), (1,)), ((), ()))


def spectral_tables(modes, local_time, total):
    phase = np.outer(np.arange(modes), np.arange(local_time)) % total
    angle = phase * (2.0 * np.pi / total)
    both = np.concatenate([np.cos(angle), np.sin(angle)], axis=0)
    return both.astype(np.float32).astype(ml_dtypes.bfloat16)


def dot(left, right):
    return jnp.dot(left, right, preferred_element_type=jnp.float32)


def dot_t(left, right):
    return lax.dot_general(left, right, NT_DIMS, preferred_element_type=jnp.float32)


def kernel(
    sizes,
    vis_hbm,
    table_hbm,
    beam_hbm,
    gain_hbm,
    basis_hbm,
    step_hbm,
    kl_hbm,
    out_ref,
    vis_v,
    table_v,
    beam_v,
    gain_v,
    basis_v,
    step_s,
    kl_v,
    send_v,
    recv_v,
    ysend_v,
    yrecv_v,
    load_sem,
    send_sem,
    recv_sem,
    pol_sem,
    freq_sem,
    pass_sem,
    y_sem,
):
    n_ma, n_pol, n_freq = sizes
    a, p, fr = lax.axis_index("ma"), lax.axis_index("pol"), lax.axis_index("freq")
    _, nfreq, nbase, ntime = vis_v.shape
    local_modes, degrees = gain_v.shape
    all_modes = local_modes * n_ma
    half = nfreq * nbase
    full = n_pol * half
    kept = kl_v.shape[0] // n_freq
    peers = [(da, dp) for da in range(n_ma) for dp in range(n_pol) if (da, dp) != (0, 0)]
    peers.sort(key=lambda o: (abs(o[0] - n_ma // 2), o[1]))

    tchunks = table_v.shape[0]
    tsize = ntime // tchunks
    spectral = []
    for i in range(tchunks):
        cols = pl.ds(i * tsize, tsize)
        group = [
            pltpu.make_async_copy(
                vis_hbm.at[:, part, :, cols], vis_v.at[part, :, :, cols], load_sem.at[3 * i + part]
            )
            for part in range(2)
        ]
        group.append(pltpu.make_async_copy(table_hbm.at[i], table_v.at[i], load_sem.at[3 * i + 2]))
        for c in group:
            c.start()
        spectral.append(group)
    loads = [
        pltpu.make_async_copy(src, dst, load_sem.at[3 * tchunks + i])
        for i, (src, dst) in enumerate(
            [
                (step_hbm, step_s),
                (kl_hbm, kl_v),
                (basis_hbm, basis_v),
                (beam_hbm, beam_v.at[fr, p]),
                (gain_hbm, gain_v),
            ]
        )
    ]
    for c in loads:
        c.start()

    barrier = pltpu.get_barrier_semaphore()

    def group_id(da, dp):
        return {"ma": lax.rem(a + da, n_ma), "pol": lax.rem(p + dp, n_pol)}

    def freq_id(df):
        return {"freq": lax.rem(fr + df, n_freq)}

    def remote(src, dst, send, recv, to):
        copy = pltpu.make_async_remote_copy(
            src_ref=src,
            dst_ref=dst,
            send_sem=send,
            recv_sem=recv,
            device_id=to,
            device_id_type=MESH,
        )
        copy.start()
        return copy

    for da, dp in peers:
        pl.semaphore_signal(barrier, inc=1, device_id=group_id(da, dp), device_id_type=MESH)
    for df in range(1, n_freq):
        pl.semaphore_signal(barrier, inc=1, device_id=freq_id(df), device_id_type=MESH)

    total = None
    for i in range(tchunks):
        for c in spectral[i]:
            c.wait()
        samples = vis_v[:, :, :, i * tsize : (i + 1) * tsize].reshape(2 * half, tsize)
        term = dot_t(table_v[i], samples)
        total = term if total is None else total + term
    cosine, sine = total[:all_modes], total[all_modes:]
    real = cosine[:, :half] + sine[:, half:]
    imag = cosine[:, half:] - sine[:, :half]
    turn = lax.rem(a * lax.broadcasted_iota(jnp.int32, (all_modes, half), 0), n_ma)
    scale = float(ntime * n_ma) ** -0.5
    pc = jnp.full((all_modes, half), scale, jnp.float32)
    ps = jnp.zeros((all_modes, half), jnp.float32)
    for r in range(1, n_ma):
        angle = 2.0 * np.pi * r / n_ma
        pc = jnp.where(turn == r, float(scale * np.cos(angle)), pc)
        ps = jnp.where(turn == r, float(scale * np.sin(angle)), ps)
    block = (n_ma, local_modes, half)
    send_v[0] = (real * pc + imag * ps).astype(jnp.bfloat16).reshape(block)
    send_v[1] = (imag * pc - real * ps).astype(jnp.bfloat16).reshape(block)

    pl.semaphore_wait(barrier, len(peers) + n_freq - 1)
    copies = []
    for i, (da, dp) in enumerate(peers):
        to = group_id(da, dp)
        src = send_v.at[to["pol"], to["ma"]]
        copies.append(remote(src, recv_v.at[p, a], send_sem.at[i], recv_sem.at[i], to))
    mine = beam_v.at[fr, p]
    pol_copies = [
        remote(beam_hbm, mine, pol_sem.at[0, d - 1], pol_sem.at[1, d - 1], group_id(0, d))
        for d in range(1, n_pol)
    ]
    freq_copies = [
        remote(beam_hbm, mine, freq_sem.at[0, d - 1], freq_sem.at[1, d - 1], freq_id(d))
        for d in range(1, n_freq)
    ]
    recv_v[p, a] = send_v[p, a]

    for c in loads:
        c.wait()
    lane = lax.rem(lax.broadcasted_iota(jnp.int32, (local_modes, full), 1), half)
    own = [(lane >= f * nbase) & (lane < (f + 1) * nbase) for f in range(nfreq)]
    mode = lax.broadcasted_iota(jnp.int32, (local_modes, degrees), 0) + a * local_modes
    keep = lax.broadcasted_iota(jnp.int32, (local_modes, degrees), 1) >= mode
    kl = kl_v[...].astype(jnp.float32)
    kl_row = lax.broadcasted_iota(jnp.int32, kl.shape, 0)
    kl_col = lax.broadcasted_iota(jnp.int32, kl.shape, 1)

    def kl_weight(j, f):
        chosen = (kl_row == j) & (kl_col == fr * nfreq + f)
        return jnp.sum(jnp.where(chosen, kl, 0.0), axis=(0, 1), keepdims=True)

    def lane_weights(df):
        weights = []
        for j in range(kept):
            row = jnp.zeros((1, full), jnp.float32)
            for f in range(nfreq):
                value = kl_weight(lax.rem(fr + df, n_freq) * kept + j, f)
                row = jnp.where(own[f][:1], value, row)
            weights.append(row)
        return weights

    weights = [lane_weights(df) for df in range(n_freq)]
    steps = jnp.zeros((1, full), jnp.float32)
    for f in range(nfreq):
        steps = jnp.where(own[f][:1], step_s[f], steps)

    for copy in pol_copies + copies:
        copy.wait_recv()

    def spread(value):
        return jnp.concatenate(
            [jnp.where(own[f], value, 0.0) for f in range(nfreq)], axis=0
        ).astype(jnp.bfloat16)

    def gather(value):
        result = jnp.zeros((local_modes, full), jnp.float32)
        for f in range(nfreq):
            result = jnp.where(own[f], value[f * local_modes : (f + 1) * local_modes], result)
        return result

    def with_gain(value):
        value = value.reshape(-1, local_modes, degrees) * gain_v[...][None]
        return value.astype(jnp.bfloat16).reshape(-1, degrees)

    def masked(value):
        value = value.reshape(-1, local_modes, degrees)
        return jnp.where(keep[None], value, 0.0).astype(jnp.bfloat16).reshape(-1, degrees)

    def again(y):
        rows = beam_v[fr].reshape(full, degrees)
        coeffs = masked(dot(with_gain(dot(spread(y), rows)), basis_v[...]))
        return gather(dot_t(with_gain(dot_t(coeffs, basis_v[...])), rows))

    halves = []
    for q in range(n_pol):
        summed = recv_v[q, 0].astype(jnp.float32)
        for s in range(1, n_ma):
            summed = summed + recv_v[q, s].astype(jnp.float32)
        halves.append(summed)
    z = steps * jnp.concatenate(halves, axis=1)
    y = z
    pass_copies = []
    for it in range(ITERS):
        y = y + z - steps * again(y)
        if it == 0:
            for d, copy in enumerate(freq_copies, 1):
                copy.wait_recv()
                slot = beam_v.at[lax.rem(fr + n_freq - d, n_freq), p]
                for dp in range(1, n_pol):
                    sems = (pass_sem.at[0, d - 1, dp - 1], pass_sem.at[1, d - 1, dp - 1])
                    pass_copies.append(remote(slot, slot, *sems, group_id(0, dp)))

    y_copies = []
    for d in range(1, n_freq):
        for j in range(kept):
            ysend_v[d - 1, j] = (y * weights[d][j]).astype(jnp.bfloat16)
        sems = (y_sem.at[0, d - 1], y_sem.at[1, d - 1])
        y_copies.append(remote(ysend_v.at[d - 1], yrecv_v.at[fr], *sems, freq_id(d)))
    for j in range(kept):
        yrecv_v[fr, j] = (y * weights[0][j]).astype(jnp.bfloat16)

    for copy in pass_copies + y_copies:
        copy.wait_recv()
    left = jnp.concatenate(
        [yrecv_v[s].reshape(kept * local_modes, full) for s in range(n_freq)], axis=1
    )
    g = dot(left, beam_v[...].reshape(n_freq * full, degrees))
    out_ref[...] = masked(dot(with_gain(g), basis_v[...])).reshape(out_ref.shape)
    for copy in copies + pol_copies + freq_copies + pass_copies + y_copies:
        copy.wait_send()


def on_device(sizes, visibility, beam_rows, mode_gain, harmonic_basis, step_size, kl_matrix):
    n_ma, n_pol, n_freq = sizes
    nfreq, _, nbase, ntime = visibility.shape
    local_modes, degrees = mode_gain.shape
    kept = kl_matrix.shape[0] // n_freq
    half = nfreq * nbase
    full = n_pol * half
    all_modes = local_modes * n_ma
    tchunks = 2 if ntime % 512 == 0 else 1
    table = spectral_tables(all_modes, ntime, ntime * n_ma)
    table = np.ascontiguousarray(table.reshape(2 * all_modes, tchunks, -1).transpose(1, 0, 2))
    peers = n_ma * n_pol - 1
    hops, cores = max(n_freq - 1, 1), max(n_pol - 1, 1)
    dma = pltpu.SemaphoreType.DMA
    out_shape = (kept, local_modes, degrees)
    out = pl.pallas_call(
        functools.partial(kernel, sizes),
        out_shape=pltpu.VMEM(out_shape, jnp.bfloat16),
        in_specs=[pl.BlockSpec(memory_space=pl.ANY)] * 7,
        out_specs=pl.BlockSpec(memory_space=pltpu.VMEM),
        scratch_shapes=[
            pltpu.VMEM((2, nfreq, nbase, ntime), jnp.bfloat16),
            pltpu.VMEM(table.shape, jnp.bfloat16),
            pltpu.VMEM((n_freq, n_pol, nfreq, nbase, degrees), jnp.bfloat16),
            pltpu.VMEM((local_modes, degrees), jnp.float32),
            pltpu.VMEM(harmonic_basis.shape, jnp.bfloat16),
            pltpu.SMEM(step_size.shape, jnp.float32),
            pltpu.VMEM(kl_matrix.shape, jnp.bfloat16),
            pltpu.VMEM((2, n_ma, local_modes, half), jnp.bfloat16),
            pltpu.VMEM((n_pol, n_ma, local_modes, half), jnp.bfloat16),
            pltpu.VMEM((hops, kept, local_modes, full), jnp.bfloat16),
            pltpu.VMEM((n_freq, kept, local_modes, full), jnp.bfloat16),
            dma((3 * tchunks + 5,)),
            dma((peers,)),
            dma((peers,)),
            dma((2, cores)),
            dma((2, hops)),
            dma((2, hops, cores)),
            dma((2, hops)),
        ],
        compiler_params=pltpu.CompilerParams(
            collective_id=0, has_side_effects=True, vmem_limit_bytes=56 * 2**20
        ),
    )(
        visibility,
        jnp.asarray(table),
        beam_rows,
        mode_gain,
        harmonic_basis,
        step_size,
        kl_matrix,
    )
    return out.transpose(1, 0, 2)[:, :, None, :]


def solution(mesh):
    sizes = (mesh.shape["ma"], mesh.shape["pol"], mesh.shape["freq"])
    placed = (
        P(("slab", "freq"), None, "pol", "ma"),
        P(("slab", "freq"), "pol", None),
        P("ma", None),
        P(),
        P(("slab", "freq")),
        P("slab", None),
    )
    return jax.shard_map(
        functools.partial(on_device, sizes),
        mesh=mesh,
        in_specs=placed,
        out_specs=P("ma", ("slab", "freq"), "pol", None),
        check_vma=False,
    )
```

```python
import functools

import jax
import jax.numpy as jnp
import ml_dtypes
import numpy as np
from jax import lax
from jax.experimental import pallas as pl
from jax.experimental.pallas import tpu as pltpu
from jax.sharding import PartitionSpec as P

ITERS = 2
MESH = pl.DeviceIdType.MESH
NT_DIMS = (((1,), (1,)), ((), ()))


def spectral_tables(modes, local_time, total):
    phase = np.outer(np.arange(modes), np.arange(local_time)) % total
    angle = phase * (2.0 * np.pi / total)
    both = np.concatenate([np.cos(angle), np.sin(angle)], axis=0)
    return both.astype(np.float32).astype(ml_dtypes.bfloat16)


def dot(left, right):
    return jnp.dot(left, right, preferred_element_type=jnp.float32)


def dot_t(left, right):
    return lax.dot_general(left, right, NT_DIMS, preferred_element_type=jnp.float32)


def kernel(
    sizes,
    vis_hbm,
    table_hbm,
    beam_hbm,
    gain_hbm,
    basis_hbm,
    step_hbm,
    kl_hbm,
    out_ref,
    vis_v,
    table_v,
    beam_v,
    gain_v,
    basis_v,
    step_s,
    kl_v,
    send_v,
    recv_v,
    ysend_v,
    yrecv_v,
    load_sem,
    send_sem,
    recv_sem,
    pol_sem,
    freq_sem,
    pass_sem,
    y_sem,
):
    n_ma, n_pol, n_freq = sizes
    a, p, fr = lax.axis_index("ma"), lax.axis_index("pol"), lax.axis_index("freq")
    _, nfreq, nbase, ntime = vis_v.shape
    local_modes, degrees = gain_v.shape
    all_modes = local_modes * n_ma
    half = nfreq * nbase
    full = n_pol * half
    kept = kl_v.shape[0] // n_freq
    pieces = 2 if n_ma % 2 == 0 else 1
    span = n_ma // pieces
    starts = [lax.rem(a // span + 1 + piece, pieces) * span for piece in range(pieces)]

    tchunks, tsize = table_v.shape[0], table_v.shape[-1]
    vis_loads, table_loads = [], [[] for _ in range(pieces)]

    def load_table(piece, i):
        part = pl.ds(starts[piece], span)
        sem = load_sem.at[tchunks * (2 + piece) + i]
        copy = pltpu.make_async_copy(table_hbm.at[i, part], table_v.at[i, part], sem)
        copy.start()
        table_loads[piece].append(copy)

    for i in range(tchunks):
        cols = pl.ds(i * tsize, tsize)
        group = [
            pltpu.make_async_copy(
                vis_hbm.at[:, part, :, cols], vis_v.at[part, :, :, cols], load_sem.at[2 * i + part]
            )
            for part in range(2)
        ]
        for c in group:
            c.start()
        vis_loads.append(group)
        load_table(0, i)
    for piece in range(1, pieces):
        for i in range(tchunks):
            load_table(piece, i)
    loads = [
        pltpu.make_async_copy(src, dst, load_sem.at[tchunks * (2 + pieces) + i])
        for i, (src, dst) in enumerate(
            [
                (step_hbm, step_s),
                (kl_hbm, kl_v),
                (beam_hbm, beam_v.at[fr, p]),
                (gain_hbm, gain_v),
                (basis_hbm, basis_v),
            ]
        )
    ]

    barrier = pltpu.get_barrier_semaphore()

    def group_id(da, dp):
        return {"ma": lax.rem(a + da, n_ma), "pol": lax.rem(p + dp, n_pol)}

    def freq_id(df):
        return {"freq": lax.rem(fr + df, n_freq)}

    def remote(src, dst, send, recv, to):
        copy = pltpu.make_async_remote_copy(
            src_ref=src,
            dst_ref=dst,
            send_sem=send,
            recv_sem=recv,
            device_id=to,
            device_id_type=MESH,
        )
        copy.start()
        return copy

    for da, dp in [(da, dp) for da in range(n_ma) for dp in range(n_pol)][1:]:
        pl.semaphore_signal(barrier, inc=1, device_id=group_id(da, dp), device_id_type=MESH)
    for df in range(1, n_freq):
        pl.semaphore_signal(barrier, inc=1, device_id=freq_id(df), device_id_type=MESH)

    scale = float(ntime * n_ma) ** -0.5
    shape = (span, local_modes, half)
    copies = []
    for piece, start in enumerate(starts):
        total = None
        for i in range(tchunks):
            if piece == 0:
                for c in vis_loads[i]:
                    c.wait()
            table_loads[piece][i].wait()
            if piece == 0 and i == tchunks - 1:
                for c in loads:
                    c.start()
            samples = vis_v[:, :, :, i * tsize : (i + 1) * tsize].reshape(2 * half, tsize)
            term = dot_t(table_v[i, pl.ds(start, span)].reshape(-1, tsize), samples)
            total = term if total is None else total + term
        total = total.reshape(span, 2, local_modes, 2 * half)
        real = total[:, 0, :, :half] + total[:, 1, :, half:]
        imag = total[:, 0, :, half:] - total[:, 1, :, :half]
        mode = lax.broadcasted_iota(jnp.int32, shape, 1) + local_modes * (
            start + lax.broadcasted_iota(jnp.int32, shape, 0)
        )
        turn = lax.rem(a * mode, n_ma)
        pc = jnp.full(shape, scale, jnp.float32)
        ps = jnp.zeros(shape, jnp.float32)
        for r in range(1, n_ma):
            angle = 2.0 * np.pi * r / n_ma
            pc = jnp.where(turn == r, float(scale * np.cos(angle)), pc)
            ps = jnp.where(turn == r, float(scale * np.sin(angle)), ps)
        send_v[0, pl.ds(start, span)] = (real * pc + imag * ps).astype(jnp.bfloat16)
        send_v[1, pl.ds(start, span)] = (imag * pc - real * ps).astype(jnp.bfloat16)

        if piece == 0:
            pl.semaphore_wait(barrier, n_ma * n_pol - 1 + n_freq - 1)
        for i in range(span):
            for dp in range(n_pol):
                if piece == pieces - 1 and (i, dp) == (0, 0):
                    continue
                to = {"ma": start + lax.rem(a + i, span), "pol": lax.rem(p + dp, n_pol)}
                src = send_v.at[to["pol"], to["ma"]]
                n = len(copies)
                copies.append(remote(src, recv_v.at[p, a], send_sem.at[n], recv_sem.at[n], to))
    mine = beam_v.at[fr, p]
    pol_copies = [
        remote(beam_hbm, mine, pol_sem.at[0, d - 1], pol_sem.at[1, d - 1], group_id(0, d))
        for d in range(1, n_pol)
    ]
    freq_copies = [
        remote(beam_hbm, mine, freq_sem.at[0, d - 1], freq_sem.at[1, d - 1], freq_id(d))
        for d in range(1, n_freq)
    ]
    recv_v[p, a] = send_v[p, a]

    for c in loads:
        c.wait()
    lane = lax.rem(lax.broadcasted_iota(jnp.int32, (local_modes, full), 1), half)
    own = [(lane >= f * nbase) & (lane < (f + 1) * nbase) for f in range(nfreq)]
    mode = lax.broadcasted_iota(jnp.int32, (local_modes, degrees), 0) + a * local_modes
    keep = lax.broadcasted_iota(jnp.int32, (local_modes, degrees), 1) >= mode
    kl = kl_v[...].astype(jnp.float32)
    kl_row = lax.broadcasted_iota(jnp.int32, kl.shape, 0)
    kl_col = lax.broadcasted_iota(jnp.int32, kl.shape, 1)

    def kl_weight(j, f):
        chosen = (kl_row == j) & (kl_col == fr * nfreq + f)
        return jnp.sum(jnp.where(chosen, kl, 0.0), axis=(0, 1), keepdims=True)

    def lane_weights(df):
        weights = []
        for j in range(kept):
            row = jnp.zeros((1, full), jnp.float32)
            for f in range(nfreq):
                value = kl_weight(lax.rem(fr + df, n_freq) * kept + j, f)
                row = jnp.where(own[f][:1], value, row)
            weights.append(row)
        return weights

    weights = [lane_weights(df) for df in range(n_freq)]
    steps = jnp.zeros((1, full), jnp.float32)
    for f in range(nfreq):
        steps = jnp.where(own[f][:1], step_s[f], steps)

    for copy in pol_copies + copies:
        copy.wait_recv()

    def spread(value):
        return jnp.concatenate(
            [jnp.where(own[f], value, 0.0) for f in range(nfreq)], axis=0
        ).astype(jnp.bfloat16)

    def gather(value):
        result = jnp.zeros((local_modes, full), jnp.float32)
        for f in range(nfreq):
            result = jnp.where(own[f], value[f * local_modes : (f + 1) * local_modes], result)
        return result

    def with_gain(value):
        value = value.reshape(-1, local_modes, degrees) * gain_v[...][None]
        return value.astype(jnp.bfloat16).reshape(-1, degrees)

    def masked(value):
        value = value.reshape(-1, local_modes, degrees)
        return jnp.where(keep[None], value, 0.0).astype(jnp.bfloat16).reshape(-1, degrees)

    def again(y):
        rows = beam_v[fr].reshape(full, degrees)
        coeffs = masked(dot(with_gain(dot(spread(y), rows)), basis_v[...]))
        return gather(dot_t(with_gain(dot_t(coeffs, basis_v[...])), rows))

    halves = []
    for q in range(n_pol):
        summed = recv_v[q, 0].astype(jnp.float32)
        for s in range(1, n_ma):
            summed = summed + recv_v[q, s].astype(jnp.float32)
        halves.append(summed)
    z = steps * jnp.concatenate(halves, axis=1)
    y = z
    pass_copies = []
    for it in range(ITERS):
        y = y + z - steps * again(y)
        if it == 0:
            for d, copy in enumerate(freq_copies, 1):
                copy.wait_recv()
                slot = beam_v.at[lax.rem(fr + n_freq - d, n_freq), p]
                for dp in range(1, n_pol):
                    sems = (pass_sem.at[0, d - 1, dp - 1], pass_sem.at[1, d - 1, dp - 1])
                    pass_copies.append(remote(slot, slot, *sems, group_id(0, dp)))

    y_copies = []
    for d in range(1, n_freq):
        for j in range(kept):
            ysend_v[d - 1, j] = (y * weights[d][j]).astype(jnp.bfloat16)
        sems = (y_sem.at[0, d - 1], y_sem.at[1, d - 1])
        y_copies.append(remote(ysend_v.at[d - 1], yrecv_v.at[d - 1], *sems, freq_id(d)))

    left = jnp.concatenate([y * w for w in weights[0]], axis=0).astype(jnp.bfloat16)
    g = dot(left, beam_v[fr].reshape(full, degrees))
    for copy in pass_copies + y_copies:
        copy.wait_recv()
    for d in range(1, n_freq):
        left = yrecv_v[d - 1].reshape(kept * local_modes, full)
        source = lax.rem(fr + n_freq - d, n_freq)
        g = g + dot(left, beam_v[source].reshape(full, degrees))
    out_ref[...] = masked(dot(with_gain(g), basis_v[...])).reshape(out_ref.shape)
    for copy in copies + pol_copies + freq_copies + pass_copies + y_copies:
        copy.wait_send()


def on_device(sizes, visibility, beam_rows, mode_gain, harmonic_basis, step_size, kl_matrix):
    n_ma, n_pol, n_freq = sizes
    nfreq, _, nbase, ntime = visibility.shape
    local_modes, degrees = mode_gain.shape
    kept = kl_matrix.shape[0] // n_freq
    half = nfreq * nbase
    full = n_pol * half
    all_modes = local_modes * n_ma
    tchunks = 2 if ntime % 512 == 0 else 1
    table = spectral_tables(all_modes, ntime, ntime * n_ma)
    table = table.reshape(2, n_ma, local_modes, tchunks, -1).transpose(3, 1, 0, 2, 4)
    table = np.ascontiguousarray(table)
    peers = n_ma * n_pol - 1
    hops, cores = max(n_freq - 1, 1), max(n_pol - 1, 1)
    dma = pltpu.SemaphoreType.DMA
    out_shape = (kept, local_modes, degrees)
    out = pl.pallas_call(
        functools.partial(kernel, sizes),
        out_shape=pltpu.VMEM(out_shape, jnp.bfloat16),
        in_specs=[pl.BlockSpec(memory_space=pl.ANY)] * 7,
        out_specs=pl.BlockSpec(memory_space=pltpu.VMEM),
        scratch_shapes=[
            pltpu.VMEM((2, nfreq, nbase, ntime), jnp.bfloat16),
            pltpu.VMEM(table.shape, jnp.bfloat16),
            pltpu.VMEM((n_freq, n_pol, nfreq, nbase, degrees), jnp.bfloat16),
            pltpu.VMEM((local_modes, degrees), jnp.float32),
            pltpu.VMEM(harmonic_basis.shape, jnp.bfloat16),
            pltpu.SMEM(step_size.shape, jnp.float32),
            pltpu.VMEM(kl_matrix.shape, jnp.bfloat16),
            pltpu.VMEM((2, n_ma, local_modes, half), jnp.bfloat16),
            pltpu.VMEM((n_pol, n_ma, local_modes, half), jnp.bfloat16),
            pltpu.VMEM((hops, kept, local_modes, full), jnp.bfloat16),
            pltpu.VMEM((hops, kept, local_modes, full), jnp.bfloat16),
            dma((4 * tchunks + 5,)),
            dma((peers,)),
            dma((peers,)),
            dma((2, cores)),
            dma((2, hops)),
            dma((2, hops, cores)),
            dma((2, hops)),
        ],
        compiler_params=pltpu.CompilerParams(
            collective_id=0, has_side_effects=True, vmem_limit_bytes=56 * 2**20
        ),
    )(
        visibility,
        jnp.asarray(table),
        beam_rows,
        mode_gain,
        harmonic_basis,
        step_size,
        kl_matrix,
    )
    return out.transpose(1, 0, 2)[:, :, None, :]


def solution(mesh):
    sizes = (mesh.shape["ma"], mesh.shape["pol"], mesh.shape["freq"])
    placed = (
        P(("slab", "freq"), None, "pol", "ma"),
        P(("slab", "freq"), "pol", None),
        P("ma", None),
        P(),
        P(("slab", "freq")),
        P("slab", None),
    )
    return jax.shard_map(
        functools.partial(on_device, sizes),
        mesh=mesh,
        in_specs=placed,
        out_specs=P("ma", ("slab", "freq"), "pol", None),
        check_vma=False,
    )
```

```python
import functools

import jax
import jax.numpy as jnp
import ml_dtypes
import numpy as np
from jax import lax
from jax.experimental import pallas as pl
from jax.experimental.pallas import tpu as pltpu
from jax.sharding import PartitionSpec as P

ITERS = 2
MESH = pl.DeviceIdType.MESH


def spectral_tables(modes, local_time, total):
    phase = np.outer(np.arange(modes), np.arange(local_time)) % total
    angle = phase * (2.0 * np.pi / total)
    both = np.concatenate([np.cos(angle), np.sin(angle)], axis=0)
    return both.astype(np.float32).astype(ml_dtypes.bfloat16)


def dot(left, right):
    return jnp.dot(left, right, preferred_element_type=jnp.float32)


def kernel(
    sizes,
    vis_hbm,
    table_hbm,
    beam_hbm,
    gain_hbm,
    basis_hbm,
    step_hbm,
    kl_hbm,
    out_ref,
    vis_v,
    table_v,
    beam_v,
    gain_v,
    basis_v,
    basis_t,
    rows_t,
    step_s,
    kl_v,
    send_v,
    recv_v,
    ysend_v,
    yrecv_v,
    load_sem,
    send_sem,
    recv_sem,
    pol_sem,
    freq_sem,
    pass_sem,
    y_sem,
):
    n_ma, n_pol, n_freq = sizes
    a, p, fr = lax.axis_index("ma"), lax.axis_index("pol"), lax.axis_index("freq")
    _, nfreq, nbase, ntime = vis_v.shape
    local_modes, degrees = gain_v.shape
    all_modes = local_modes * n_ma
    half = nfreq * nbase
    full = n_pol * half
    kept = kl_v.shape[0] // n_freq
    peers = [(da, dp) for da in range(n_ma) for dp in range(n_pol) if (da, dp) != (0, 0)]
    peers.sort(key=lambda o: (abs(o[0] - n_ma // 2), o[1]))

    tchunks = table_v.shape[0]
    tsize = ntime // tchunks
    spectral = []
    for i in range(tchunks):
        cols = pl.ds(i * tsize, tsize)
        group = [
            pltpu.make_async_copy(
                vis_hbm.at[:, part, :, cols], vis_v.at[part, :, :, cols], load_sem.at[3 * i + part]
            )
            for part in range(2)
        ]
        group.append(pltpu.make_async_copy(table_hbm.at[i], table_v.at[i], load_sem.at[3 * i + 2]))
        for c in group:
            c.start()
        spectral.append(group)
    loads = [
        pltpu.make_async_copy(src, dst, load_sem.at[3 * tchunks + i])
        for i, (src, dst) in enumerate(
            [
                (step_hbm, step_s),
                (kl_hbm, kl_v),
                (basis_hbm, basis_v),
                (beam_hbm, beam_v.at[fr, p]),
                (gain_hbm, gain_v),
            ]
        )
    ]
    for c in loads:
        c.start()

    barrier = pltpu.get_barrier_semaphore()

    def group_id(da, dp):
        return {"ma": lax.rem(a + da, n_ma), "pol": lax.rem(p + dp, n_pol)}

    def freq_id(df):
        return {"freq": lax.rem(fr + df, n_freq)}

    def remote(src, dst, send, recv, to):
        copy = pltpu.make_async_remote_copy(
            src_ref=src,
            dst_ref=dst,
            send_sem=send,
            recv_sem=recv,
            device_id=to,
            device_id_type=MESH,
        )
        copy.start()
        return copy

    for da, dp in peers:
        pl.semaphore_signal(barrier, inc=1, device_id=group_id(da, dp), device_id_type=MESH)
    for df in range(1, n_freq):
        pl.semaphore_signal(barrier, inc=1, device_id=freq_id(df), device_id_type=MESH)

    total = None
    for i in range(tchunks):
        for c in spectral[i]:
            c.wait()
        samples = vis_v[:, :, :, i * tsize : (i + 1) * tsize].reshape(2 * half, tsize)
        term = dot(samples, table_v[i])
        total = term if total is None else total + term
    total = total.T
    cosine, sine = total[:all_modes], total[all_modes:]
    real = cosine[:, :half] + sine[:, half:]
    imag = cosine[:, half:] - sine[:, :half]
    turn = lax.rem(a * lax.broadcasted_iota(jnp.int32, (all_modes, half), 0), n_ma)
    scale = float(ntime * n_ma) ** -0.5
    pc = jnp.full((all_modes, half), scale, jnp.float32)
    ps = jnp.zeros((all_modes, half), jnp.float32)
    for r in range(1, n_ma):
        angle = 2.0 * np.pi * r / n_ma
        pc = jnp.where(turn == r, float(scale * np.cos(angle)), pc)
        ps = jnp.where(turn == r, float(scale * np.sin(angle)), ps)
    block = (n_ma, local_modes, half)
    send_v[0] = (real * pc + imag * ps).astype(jnp.bfloat16).reshape(block)
    send_v[1] = (imag * pc - real * ps).astype(jnp.bfloat16).reshape(block)

    pl.semaphore_wait(barrier, len(peers) + n_freq - 1)
    copies = []
    for i, (da, dp) in enumerate(peers):
        to = group_id(da, dp)
        src = send_v.at[to["pol"], to["ma"]]
        copies.append(remote(src, recv_v.at[p, a], send_sem.at[i], recv_sem.at[i], to))
    mine = beam_v.at[fr, p]
    pol_copies = [
        remote(beam_hbm, mine, pol_sem.at[0, d - 1], pol_sem.at[1, d - 1], group_id(0, d))
        for d in range(1, n_pol)
    ]
    freq_copies = [
        remote(beam_hbm, mine, freq_sem.at[0, d - 1], freq_sem.at[1, d - 1], freq_id(d))
        for d in range(1, n_freq)
    ]
    recv_v[p, a] = send_v[p, a]

    for c in loads:
        c.wait()
    lane = lax.rem(lax.broadcasted_iota(jnp.int32, (local_modes, full), 1), half)
    own = [(lane >= f * nbase) & (lane < (f + 1) * nbase) for f in range(nfreq)]
    mode = lax.broadcasted_iota(jnp.int32, (local_modes, degrees), 0) + a * local_modes
    keep = lax.broadcasted_iota(jnp.int32, (local_modes, degrees), 1) >= mode
    kl = kl_v[...].astype(jnp.float32)
    kl_row = lax.broadcasted_iota(jnp.int32, kl.shape, 0)
    kl_col = lax.broadcasted_iota(jnp.int32, kl.shape, 1)

    def kl_weight(j, f):
        chosen = (kl_row == j) & (kl_col == fr * nfreq + f)
        return jnp.sum(jnp.where(chosen, kl, 0.0), axis=(0, 1), keepdims=True)

    def lane_weights(df):
        weights = []
        for j in range(kept):
            row = jnp.zeros((1, full), jnp.float32)
            for f in range(nfreq):
                value = kl_weight(lax.rem(fr + df, n_freq) * kept + j, f)
                row = jnp.where(own[f][:1], value, row)
            weights.append(row)
        return weights

    weights = [lane_weights(df) for df in range(n_freq)]
    steps = jnp.zeros((1, full), jnp.float32)
    for f in range(nfreq):
        steps = jnp.where(own[f][:1], step_s[f], steps)

    basis_t[...] = basis_v[...].T
    for copy in pol_copies:
        copy.wait_recv()
    rows_t[...] = beam_v[fr].reshape(full, degrees).T
    for copy in copies:
        copy.wait_recv()

    def spread(value):
        return jnp.concatenate(
            [jnp.where(own[f], value, 0.0) for f in range(nfreq)], axis=0
        ).astype(jnp.bfloat16)

    def gather(value):
        result = jnp.zeros((local_modes, full), jnp.float32)
        for f in range(nfreq):
            result = jnp.where(own[f], value[f * local_modes : (f + 1) * local_modes], result)
        return result

    def with_gain(value):
        value = value.reshape(-1, local_modes, degrees) * gain_v[...][None]
        return value.astype(jnp.bfloat16).reshape(-1, degrees)

    def masked(value):
        value = value.reshape(-1, local_modes, degrees)
        return jnp.where(keep[None], value, 0.0).astype(jnp.bfloat16).reshape(-1, degrees)

    def again(y):
        rows = beam_v[fr].reshape(full, degrees)
        coeffs = masked(dot(with_gain(dot(spread(y), rows)), basis_v[...]))
        return gather(dot(with_gain(dot(coeffs, basis_t[...])), rows_t[...]))

    halves = []
    for q in range(n_pol):
        summed = recv_v[q, 0].astype(jnp.float32)
        for s in range(1, n_ma):
            summed = summed + recv_v[q, s].astype(jnp.float32)
        halves.append(summed)
    z = steps * jnp.concatenate(halves, axis=1)
    y = z
    pass_copies = []
    for it in range(ITERS):
        y = y + z - steps * again(y)
        if it == 0:
            for d, copy in enumerate(freq_copies, 1):
                copy.wait_recv()
                slot = beam_v.at[lax.rem(fr + n_freq - d, n_freq), p]
                for dp in range(1, n_pol):
                    sems = (pass_sem.at[0, d - 1, dp - 1], pass_sem.at[1, d - 1, dp - 1])
                    pass_copies.append(remote(slot, slot, *sems, group_id(0, dp)))

    y_copies = []
    for d in range(1, n_freq):
        for j in range(kept):
            ysend_v[d - 1, j] = (y * weights[d][j]).astype(jnp.bfloat16)
        sems = (y_sem.at[0, d - 1], y_sem.at[1, d - 1])
        y_copies.append(remote(ysend_v.at[d - 1], yrecv_v.at[d - 1], *sems, freq_id(d)))

    left = jnp.concatenate([y * w for w in weights[0]], axis=0).astype(jnp.bfloat16)
    g = dot(left, beam_v[fr].reshape(full, degrees))
    for copy in pass_copies + y_copies:
        copy.wait_recv()
    for d in range(1, n_freq):
        left = yrecv_v[d - 1].reshape(kept * local_modes, full)
        source = lax.rem(fr + n_freq - d, n_freq)
        g = g + dot(left, beam_v[source].reshape(full, degrees))
    out_ref[...] = masked(dot(with_gain(g), basis_v[...])).reshape(out_ref.shape)
    for copy in copies + pol_copies + freq_copies + pass_copies + y_copies:
        copy.wait_send()


def on_device(sizes, visibility, beam_rows, mode_gain, harmonic_basis, step_size, kl_matrix):
    n_ma, n_pol, n_freq = sizes
    nfreq, _, nbase, ntime = visibility.shape
    local_modes, degrees = mode_gain.shape
    kept = kl_matrix.shape[0] // n_freq
    half = nfreq * nbase
    full = n_pol * half
    all_modes = local_modes * n_ma
    tchunks = 2 if ntime % 512 == 0 else 1
    table = spectral_tables(all_modes, ntime, ntime * n_ma)
    table = np.ascontiguousarray(table.T).reshape(tchunks, -1, 2 * all_modes)
    peers = n_ma * n_pol - 1
    hops, cores = max(n_freq - 1, 1), max(n_pol - 1, 1)
    dma = pltpu.SemaphoreType.DMA
    out_shape = (kept, local_modes, degrees)
    out = pl.pallas_call(
        functools.partial(kernel, sizes),
        out_shape=pltpu.VMEM(out_shape, jnp.bfloat16),
        in_specs=[pl.BlockSpec(memory_space=pl.ANY)] * 7,
        out_specs=pl.BlockSpec(memory_space=pltpu.VMEM),
        scratch_shapes=[
            pltpu.VMEM((2, nfreq, nbase, ntime), jnp.bfloat16),
            pltpu.VMEM(table.shape, jnp.bfloat16),
            pltpu.VMEM((n_freq, n_pol, nfreq, nbase, degrees), jnp.bfloat16),
            pltpu.VMEM((local_modes, degrees), jnp.float32),
            pltpu.VMEM(harmonic_basis.shape, jnp.bfloat16),
            pltpu.VMEM(harmonic_basis.shape[::-1], jnp.bfloat16),
            pltpu.VMEM((degrees, full), jnp.bfloat16),
            pltpu.SMEM(step_size.shape, jnp.float32),
            pltpu.VMEM(kl_matrix.shape, jnp.bfloat16),
            pltpu.VMEM((2, n_ma, local_modes, half), jnp.bfloat16),
            pltpu.VMEM((n_pol, n_ma, local_modes, half), jnp.bfloat16),
            pltpu.VMEM((hops, kept, local_modes, full), jnp.bfloat16),
            pltpu.VMEM((hops, kept, local_modes, full), jnp.bfloat16),
            dma((3 * tchunks + 5,)),
            dma((peers,)),
            dma((peers,)),
            dma((2, cores)),
            dma((2, hops)),
            dma((2, hops, cores)),
            dma((2, hops)),
        ],
        compiler_params=pltpu.CompilerParams(
            collective_id=0, has_side_effects=True, vmem_limit_bytes=56 * 2**20
        ),
    )(
        visibility,
        jnp.asarray(table),
        beam_rows,
        mode_gain,
        harmonic_basis,
        step_size,
        kl_matrix,
    )
    return out.transpose(1, 0, 2)[:, :, None, :]


def solution(mesh):
    sizes = (mesh.shape["ma"], mesh.shape["pol"], mesh.shape["freq"])
    placed = (
        P(("slab", "freq"), None, "pol", "ma"),
        P(("slab", "freq"), "pol", None),
        P("ma", None),
        P(),
        P(("slab", "freq")),
        P("slab", None),
    )
    return jax.shard_map(
        functools.partial(on_device, sizes),
        mesh=mesh,
        in_specs=placed,
        out_specs=P("ma", ("slab", "freq"), "pol", None),
        check_vma=False,
    )
```

```python
import functools

import jax
import jax.numpy as jnp
import ml_dtypes
import numpy as np
from jax import lax
from jax.experimental import pallas as pl
from jax.experimental.pallas import tpu as pltpu
from jax.sharding import PartitionSpec as P

ITERS = 2
MESH = pl.DeviceIdType.MESH


def spectral_tables(modes, times, total):
    phase = np.outer(np.arange(times), np.arange(modes)) % total
    angle = phase * (2.0 * np.pi / total)
    both = np.zeros((times, 2, -(-modes // 128) * 128), np.float32)
    both[:, 0, :modes], both[:, 1, :modes] = np.cos(angle), np.sin(angle)
    return both.reshape(times, -1).astype(ml_dtypes.bfloat16)


def dot(left, right):
    return jnp.dot(left, right, preferred_element_type=jnp.float32)


def kernel(
    sizes,
    vis_hbm,
    table_hbm,
    beam_hbm,
    gain_hbm,
    basis_hbm,
    step_hbm,
    kl_hbm,
    out_ref,
    vis_v,
    table_v,
    beam_v,
    gain_v,
    basis_v,
    basis_t,
    rows_t,
    step_s,
    kl_v,
    send_v,
    recv_v,
    ysend_v,
    yrecv_v,
    load_sem,
    send_sem,
    recv_sem,
    pol_sem,
    freq_sem,
    pass_sem,
    y_sem,
):
    n_ma, n_pol, n_freq = sizes
    a, p, fr = lax.axis_index("ma"), lax.axis_index("pol"), lax.axis_index("freq")
    _, nfreq, nbase, ntime = vis_v.shape
    local_modes, degrees = gain_v.shape
    all_modes = local_modes * n_ma
    half = nfreq * nbase
    full = n_pol * half
    kept = kl_v.shape[0] // n_freq
    peers = [(da, dp) for da in range(n_ma) for dp in range(n_pol) if (da, dp) != (0, 0)]
    peers.sort(key=lambda o: (abs(o[0] - n_ma // 2), o[1]))

    tsize, lanes = table_v.shape[0], table_v.shape[1] // 2
    tchunks = ntime // tsize
    load_table = pltpu.make_async_copy(table_hbm, table_v, load_sem.at[2 * tchunks])
    vis_loads = []
    for i in range(tchunks):
        cols = pl.ds(i * tsize, tsize)
        group = [
            pltpu.make_async_copy(
                vis_hbm.at[:, part, :, cols], vis_v.at[part, :, :, cols], load_sem.at[2 * i + part]
            )
            for part in range(2)
        ]
        for c in group:
            c.start()
        if i == 0:
            load_table.start()
        vis_loads.append(group)
    loads = [
        pltpu.make_async_copy(src, dst, load_sem.at[2 * tchunks + 1 + i])
        for i, (src, dst) in enumerate(
            [
                (step_hbm, step_s),
                (kl_hbm, kl_v),
                (basis_hbm, basis_v),
                (beam_hbm, beam_v.at[fr, p]),
                (gain_hbm, gain_v),
            ]
        )
    ]
    for c in loads:
        c.start()

    barrier = pltpu.get_barrier_semaphore()

    def group_id(da, dp):
        return {"ma": lax.rem(a + da, n_ma), "pol": lax.rem(p + dp, n_pol)}

    def freq_id(df):
        return {"freq": lax.rem(fr + df, n_freq)}

    def remote(src, dst, send, recv, to):
        copy = pltpu.make_async_remote_copy(
            src_ref=src,
            dst_ref=dst,
            send_sem=send,
            recv_sem=recv,
            device_id=to,
            device_id_type=MESH,
        )
        copy.start()
        return copy

    for da, dp in peers:
        pl.semaphore_signal(barrier, inc=1, device_id=group_id(da, dp), device_id_type=MESH)
    for df in range(1, n_freq):
        pl.semaphore_signal(barrier, inc=1, device_id=freq_id(df), device_id_type=MESH)

    scale = float(ntime * n_ma) ** -0.5
    order = n_ma * tchunks
    mode = lax.broadcasted_iota(jnp.int32, (1, lanes), 1)
    real = imag = 0.0
    for i in range(tchunks):
        turn = lax.rem((a * tchunks + i) * mode, order)
        pc = jnp.full((1, lanes), scale, jnp.float32)
        ps = jnp.zeros((1, lanes), jnp.float32)
        for r in range(1, order):
            angle = 2.0 * np.pi * r / order
            pc = jnp.where(turn == r, float(scale * np.cos(angle)), pc)
            ps = jnp.where(turn == r, float(scale * np.sin(angle)), ps)
        for c in vis_loads[i]:
            c.wait()
        if i == 0:
            load_table.wait()
        samples = vis_v[:, :, :, i * tsize : (i + 1) * tsize].reshape(2 * half, tsize)
        total = dot(samples, table_v[...])
        first = total[:half, :lanes] + total[half:, lanes:]
        second = total[half:, :lanes] - total[:half, lanes:]
        real = real + (first * pc + second * ps)
        imag = imag + (second * pc - first * ps)
    block = (n_ma, local_modes, half)
    send_v[0] = real.T[:all_modes].astype(jnp.bfloat16).reshape(block)
    send_v[1] = imag.T[:all_modes].astype(jnp.bfloat16).reshape(block)

    pl.semaphore_wait(barrier, len(peers) + n_freq - 1)
    copies = []
    for i, (da, dp) in enumerate(peers):
        to = group_id(da, dp)
        src = send_v.at[to["pol"], to["ma"]]
        copies.append(remote(src, recv_v.at[p, a], send_sem.at[i], recv_sem.at[i], to))
    mine = beam_v.at[fr, p]
    pol_copies = [
        remote(beam_hbm, mine, pol_sem.at[0, d - 1], pol_sem.at[1, d - 1], group_id(0, d))
        for d in range(1, n_pol)
    ]
    freq_copies = [
        remote(beam_hbm, mine, freq_sem.at[0, d - 1], freq_sem.at[1, d - 1], freq_id(d))
        for d in range(1, n_freq)
    ]
    recv_v[p, a] = send_v[p, a]

    for c in loads:
        c.wait()
    lane = lax.rem(lax.broadcasted_iota(jnp.int32, (local_modes, full), 1), half)
    own = [(lane >= f * nbase) & (lane < (f + 1) * nbase) for f in range(nfreq)]
    mode = lax.broadcasted_iota(jnp.int32, (local_modes, degrees), 0) + a * local_modes
    keep = lax.broadcasted_iota(jnp.int32, (local_modes, degrees), 1) >= mode
    kl = kl_v[...].astype(jnp.float32)
    kl_row = lax.broadcasted_iota(jnp.int32, kl.shape, 0)
    kl_col = lax.broadcasted_iota(jnp.int32, kl.shape, 1)

    def kl_weight(j, f):
        chosen = (kl_row == j) & (kl_col == fr * nfreq + f)
        return jnp.sum(jnp.where(chosen, kl, 0.0), axis=(0, 1), keepdims=True)

    def lane_weights(df):
        weights = []
        for j in range(kept):
            row = jnp.zeros((1, full), jnp.float32)
            for f in range(nfreq):
                value = kl_weight(lax.rem(fr + df, n_freq) * kept + j, f)
                row = jnp.where(own[f][:1], value, row)
            weights.append(row)
        return weights

    weights = [lane_weights(df) for df in range(n_freq)]
    steps = jnp.zeros((1, full), jnp.float32)
    for f in range(nfreq):
        steps = jnp.where(own[f][:1], step_s[f], steps)

    basis_t[...] = basis_v[...].T
    for copy in pol_copies:
        copy.wait_recv()
    rows_t[...] = beam_v[fr].reshape(full, degrees).T
    for copy in copies:
        copy.wait_recv()

    def spread(value):
        return jnp.concatenate(
            [jnp.where(own[f], value, 0.0) for f in range(nfreq)], axis=0
        ).astype(jnp.bfloat16)

    def gather(value):
        result = jnp.zeros((local_modes, full), jnp.float32)
        for f in range(nfreq):
            result = jnp.where(own[f], value[f * local_modes : (f + 1) * local_modes], result)
        return result

    def with_gain(value):
        value = value.reshape(-1, local_modes, degrees) * gain_v[...][None]
        return value.astype(jnp.bfloat16).reshape(-1, degrees)

    def masked(value):
        value = value.reshape(-1, local_modes, degrees)
        return jnp.where(keep[None], value, 0.0).astype(jnp.bfloat16).reshape(-1, degrees)

    def again(y):
        rows = beam_v[fr].reshape(full, degrees)
        coeffs = masked(dot(with_gain(dot(spread(y), rows)), basis_v[...]))
        return gather(dot(with_gain(dot(coeffs, basis_t[...])), rows_t[...]))

    halves = []
    for q in range(n_pol):
        summed = recv_v[q, 0].astype(jnp.float32)
        for s in range(1, n_ma):
            summed = summed + recv_v[q, s].astype(jnp.float32)
        halves.append(summed)
    z = steps * jnp.concatenate(halves, axis=1)
    y = z
    pass_copies = []
    for it in range(ITERS):
        y = y + z - steps * again(y)
        if it == 0:
            for d, copy in enumerate(freq_copies, 1):
                copy.wait_recv()
                slot = beam_v.at[lax.rem(fr + n_freq - d, n_freq), p]
                for dp in range(1, n_pol):
                    sems = (pass_sem.at[0, d - 1, dp - 1], pass_sem.at[1, d - 1, dp - 1])
                    pass_copies.append(remote(slot, slot, *sems, group_id(0, dp)))

    y_copies = []
    for d in range(1, n_freq):
        for j in range(kept):
            ysend_v[d - 1, j] = (y * weights[d][j]).astype(jnp.bfloat16)
        sems = (y_sem.at[0, d - 1], y_sem.at[1, d - 1])
        y_copies.append(remote(ysend_v.at[d - 1], yrecv_v.at[d - 1], *sems, freq_id(d)))

    left = jnp.concatenate([y * w for w in weights[0]], axis=0).astype(jnp.bfloat16)
    g = dot(left, beam_v[fr].reshape(full, degrees))
    for copy in pass_copies + y_copies:
        copy.wait_recv()
    for d in range(1, n_freq):
        left = yrecv_v[d - 1].reshape(kept * local_modes, full)
        source = lax.rem(fr + n_freq - d, n_freq)
        g = g + dot(left, beam_v[source].reshape(full, degrees))
    out_ref[...] = masked(dot(with_gain(g), basis_v[...])).reshape(out_ref.shape)
    for copy in copies + pol_copies + freq_copies + pass_copies + y_copies:
        copy.wait_send()


def on_device(sizes, visibility, beam_rows, mode_gain, harmonic_basis, step_size, kl_matrix):
    n_ma, n_pol, n_freq = sizes
    nfreq, _, nbase, ntime = visibility.shape
    local_modes, degrees = mode_gain.shape
    kept = kl_matrix.shape[0] // n_freq
    half = nfreq * nbase
    full = n_pol * half
    all_modes = local_modes * n_ma
    tchunks = 4 if ntime % 1024 == 0 else 1
    table = spectral_tables(all_modes, ntime // tchunks, ntime * n_ma)
    peers = n_ma * n_pol - 1
    hops, cores = max(n_freq - 1, 1), max(n_pol - 1, 1)
    dma = pltpu.SemaphoreType.DMA
    out_shape = (kept, local_modes, degrees)
    out = pl.pallas_call(
        functools.partial(kernel, sizes),
        out_shape=pltpu.VMEM(out_shape, jnp.bfloat16),
        in_specs=[pl.BlockSpec(memory_space=pl.ANY)] * 7,
        out_specs=pl.BlockSpec(memory_space=pltpu.VMEM),
        scratch_shapes=[
            pltpu.VMEM((2, nfreq, nbase, ntime), jnp.bfloat16),
            pltpu.VMEM(table.shape, jnp.bfloat16),
            pltpu.VMEM((n_freq, n_pol, nfreq, nbase, degrees), jnp.bfloat16),
            pltpu.VMEM((local_modes, degrees), jnp.float32),
            pltpu.VMEM(harmonic_basis.shape, jnp.bfloat16),
            pltpu.VMEM(harmonic_basis.shape[::-1], jnp.bfloat16),
            pltpu.VMEM((degrees, full), jnp.bfloat16),
            pltpu.SMEM(step_size.shape, jnp.float32),
            pltpu.VMEM(kl_matrix.shape, jnp.bfloat16),
            pltpu.VMEM((2, n_ma, local_modes, half), jnp.bfloat16),
            pltpu.VMEM((n_pol, n_ma, local_modes, half), jnp.bfloat16),
            pltpu.VMEM((hops, kept, local_modes, full), jnp.bfloat16),
            pltpu.VMEM((hops, kept, local_modes, full), jnp.bfloat16),
            dma((2 * tchunks + 6,)),
            dma((peers,)),
            dma((peers,)),
            dma((2, cores)),
            dma((2, hops)),
            dma((2, hops, cores)),
            dma((2, hops)),
        ],
        compiler_params=pltpu.CompilerParams(
            collective_id=0, has_side_effects=True, vmem_limit_bytes=56 * 2**20
        ),
    )(
        visibility,
        jnp.asarray(table),
        beam_rows,
        mode_gain,
        harmonic_basis,
        step_size,
        kl_matrix,
    )
    return out.transpose(1, 0, 2)[:, :, None, :]


def solution(mesh):
    sizes = (mesh.shape["ma"], mesh.shape["pol"], mesh.shape["freq"])
    placed = (
        P(("slab", "freq"), None, "pol", "ma"),
        P(("slab", "freq"), "pol", None),
        P("ma", None),
        P(),
        P(("slab", "freq")),
        P("slab", None),
    )
    return jax.shard_map(
        functools.partial(on_device, sizes),
        mesh=mesh,
        in_specs=placed,
        out_specs=P("ma", ("slab", "freq"), "pol", None),
        check_vma=False,
    )
```

```python
import functools

import jax
import jax.numpy as jnp
import ml_dtypes
import numpy as np
from jax import lax
from jax.experimental import pallas as pl
from jax.experimental.pallas import tpu as pltpu
from jax.sharding import PartitionSpec as P

ITERS = 2
MESH = pl.DeviceIdType.MESH


def spectral_tables(modes, local_time, total):
    phase = np.outer(np.arange(modes), np.arange(local_time)) % total
    angle = phase * (2.0 * np.pi / total)
    both = np.concatenate([np.cos(angle), np.sin(angle)], axis=0)
    return both.astype(np.float32).astype(ml_dtypes.bfloat16)


def dot(left, right):
    return jnp.dot(left, right, preferred_element_type=jnp.float32)


def kernel(
    sizes,
    vis_hbm,
    table_hbm,
    beam_hbm,
    gain_hbm,
    basis_hbm,
    step_hbm,
    kl_hbm,
    out_ref,
    vis_v,
    table_v,
    beam_v,
    gain_v,
    basis_v,
    basis_t,
    rows_t,
    step_s,
    kl_v,
    send_v,
    recv_v,
    ysend_v,
    yrecv_v,
    load_sem,
    send_sem,
    recv_sem,
    pol_sem,
    freq_sem,
    pass_sem,
    y_sem,
):
    n_ma, n_pol, n_freq = sizes
    a, p, fr = lax.axis_index("ma"), lax.axis_index("pol"), lax.axis_index("freq")
    _, nfreq, nbase, ntime = vis_v.shape
    local_modes, degrees = gain_v.shape
    all_modes = local_modes * n_ma
    half = nfreq * nbase
    full = n_pol * half
    kept = kl_v.shape[0] // n_freq
    peers = [(da, dp) for da in range(n_ma) for dp in range(n_pol) if (da, dp) != (0, 0)]
    peers.sort(key=lambda o: (abs(o[0] - n_ma // 2), o[1]))

    barrier = pltpu.get_barrier_semaphore()

    def group_id(da, dp):
        return {"ma": lax.rem(a + da, n_ma), "pol": lax.rem(p + dp, n_pol)}

    def freq_id(df):
        return {"freq": lax.rem(fr + df, n_freq)}

    def remote(src, dst, send, recv, to):
        copy = pltpu.make_async_remote_copy(
            src_ref=src,
            dst_ref=dst,
            send_sem=send,
            recv_sem=recv,
            device_id=to,
            device_id_type=MESH,
        )
        copy.start()
        return copy

    for da, dp in peers:
        pl.semaphore_signal(barrier, inc=1, device_id=group_id(da, dp), device_id_type=MESH)
    for df in range(1, n_freq):
        pl.semaphore_signal(barrier, inc=1, device_id=freq_id(df), device_id_type=MESH)

    tchunks = table_v.shape[0]
    tsize = ntime // tchunks
    spectral = []
    for i in range(tchunks):
        cols = pl.ds(i * tsize, tsize)
        group = [
            pltpu.make_async_copy(
                vis_hbm.at[:, part, :, cols], vis_v.at[part, :, :, cols], load_sem.at[3 * i + part]
            )
            for part in range(2)
        ]
        group.append(pltpu.make_async_copy(table_hbm.at[i], table_v.at[i], load_sem.at[3 * i + 2]))
        for c in group:
            c.start()
        spectral.append(group)
    loads = [
        pltpu.make_async_copy(src, dst, load_sem.at[3 * tchunks + i])
        for i, (src, dst) in enumerate(
            [
                (step_hbm, step_s),
                (kl_hbm, kl_v),
                (basis_hbm, basis_v),
                (beam_hbm, beam_v.at[fr, p]),
                (gain_hbm, gain_v),
            ]
        )
    ]
    for c in loads:
        c.start()

    total = None
    for i in range(tchunks):
        for c in spectral[i]:
            c.wait()
        samples = vis_v[:, :, :, i * tsize : (i + 1) * tsize].reshape(2 * half, tsize)
        term = dot(samples, table_v[i])
        total = term if total is None else total + term
        if i == 0:
            pl.semaphore_wait(barrier, len(peers) + n_freq - 1)
            mine = beam_v.at[fr, p]
            pol_copies = [
                remote(beam_hbm, mine, pol_sem.at[0, d - 1], pol_sem.at[1, d - 1], group_id(0, d))
                for d in range(1, n_pol)
            ]
            freq_copies = [
                remote(beam_hbm, mine, freq_sem.at[0, d - 1], freq_sem.at[1, d - 1], freq_id(d))
                for d in range(1, n_freq)
            ]
    total = total.T
    cosine, sine = total[:all_modes], total[all_modes:]
    real = cosine[:, :half] + sine[:, half:]
    imag = cosine[:, half:] - sine[:, :half]
    turn = lax.rem(a * lax.broadcasted_iota(jnp.int32, (all_modes, half), 0), n_ma)
    scale = float(ntime * n_ma) ** -0.5
    pc = jnp.full((all_modes, half), scale, jnp.float32)
    ps = jnp.zeros((all_modes, half), jnp.float32)
    for r in range(1, n_ma):
        angle = 2.0 * np.pi * r / n_ma
        pc = jnp.where(turn == r, float(scale * np.cos(angle)), pc)
        ps = jnp.where(turn == r, float(scale * np.sin(angle)), ps)
    block = (n_ma, local_modes, half)
    send_v[0] = (real * pc + imag * ps).astype(jnp.bfloat16).reshape(block)
    send_v[1] = (imag * pc - real * ps).astype(jnp.bfloat16).reshape(block)

    copies = []
    for i, (da, dp) in enumerate(peers):
        to = group_id(da, dp)
        src = send_v.at[to["pol"], to["ma"]]
        copies.append(remote(src, recv_v.at[p, a], send_sem.at[i], recv_sem.at[i], to))
    recv_v[p, a] = send_v[p, a]

    for c in loads:
        c.wait()
    lane = lax.rem(lax.broadcasted_iota(jnp.int32, (local_modes, full), 1), half)
    own = [(lane >= f * nbase) & (lane < (f + 1) * nbase) for f in range(nfreq)]
    mode = lax.broadcasted_iota(jnp.int32, (local_modes, degrees), 0) + a * local_modes
    keep = lax.broadcasted_iota(jnp.int32, (local_modes, degrees), 1) >= mode
    kl = kl_v[...].astype(jnp.float32)
    kl_row = lax.broadcasted_iota(jnp.int32, kl.shape, 0)
    kl_col = lax.broadcasted_iota(jnp.int32, kl.shape, 1)

    def kl_weight(j, f):
        chosen = (kl_row == j) & (kl_col == fr * nfreq + f)
        return jnp.sum(jnp.where(chosen, kl, 0.0), axis=(0, 1), keepdims=True)

    def lane_weights(df):
        weights = []
        for j in range(kept):
            row = jnp.zeros((1, full), jnp.float32)
            for f in range(nfreq):
                value = kl_weight(lax.rem(fr + df, n_freq) * kept + j, f)
                row = jnp.where(own[f][:1], value, row)
            weights.append(row)
        return weights

    weights = [lane_weights(df) for df in range(n_freq)]
    steps = jnp.zeros((1, full), jnp.float32)
    for f in range(nfreq):
        steps = jnp.where(own[f][:1], step_s[f], steps)

    basis_t[...] = basis_v[...].T
    for copy in pol_copies:
        copy.wait_recv()
    rows_t[...] = beam_v[fr].reshape(full, degrees).T
    for copy in copies:
        copy.wait_recv()

    def spread(value):
        return jnp.concatenate(
            [jnp.where(own[f], value, 0.0) for f in range(nfreq)], axis=0
        ).astype(jnp.bfloat16)

    def gather(value):
        result = jnp.zeros((local_modes, full), jnp.float32)
        for f in range(nfreq):
            result = jnp.where(own[f], value[f * local_modes : (f + 1) * local_modes], result)
        return result

    def with_gain(value):
        value = value.reshape(-1, local_modes, degrees) * gain_v[...][None]
        return value.astype(jnp.bfloat16).reshape(-1, degrees)

    def masked(value):
        value = value.reshape(-1, local_modes, degrees)
        return jnp.where(keep[None], value, 0.0).astype(jnp.bfloat16).reshape(-1, degrees)

    def again(y):
        rows = beam_v[fr].reshape(full, degrees)
        coeffs = masked(dot(with_gain(dot(spread(y), rows)), basis_v[...]))
        return gather(dot(with_gain(dot(coeffs, basis_t[...])), rows_t[...]))

    halves = []
    for q in range(n_pol):
        summed = recv_v[q, 0].astype(jnp.float32)
        for s in range(1, n_ma):
            summed = summed + recv_v[q, s].astype(jnp.float32)
        halves.append(summed)
    z = steps * jnp.concatenate(halves, axis=1)
    y = z
    pass_copies = []
    for it in range(ITERS):
        y = y + z - steps * again(y)
        if it == 0:
            for d, copy in enumerate(freq_copies, 1):
                copy.wait_recv()
                slot = beam_v.at[lax.rem(fr + n_freq - d, n_freq), p]
                for dp in range(1, n_pol):
                    sems = (pass_sem.at[0, d - 1, dp - 1], pass_sem.at[1, d - 1, dp - 1])
                    pass_copies.append(remote(slot, slot, *sems, group_id(0, dp)))

    y_copies = []
    for d in range(1, n_freq):
        for j in range(kept):
            ysend_v[d - 1, j] = (y * weights[d][j]).astype(jnp.bfloat16)
        sems = (y_sem.at[0, d - 1], y_sem.at[1, d - 1])
        y_copies.append(remote(ysend_v.at[d - 1], yrecv_v.at[d - 1], *sems, freq_id(d)))

    left = jnp.concatenate([y * w for w in weights[0]], axis=0).astype(jnp.bfloat16)
    g = dot(left, beam_v[fr].reshape(full, degrees))
    for copy in pass_copies + y_copies:
        copy.wait_recv()
    for d in range(1, n_freq):
        left = yrecv_v[d - 1].reshape(kept * local_modes, full)
        source = lax.rem(fr + n_freq - d, n_freq)
        g = g + dot(left, beam_v[source].reshape(full, degrees))
    out_ref[...] = masked(dot(with_gain(g), basis_v[...])).reshape(out_ref.shape)
    for copy in copies + pol_copies + freq_copies + pass_copies + y_copies:
        copy.wait_send()


def on_device(sizes, visibility, beam_rows, mode_gain, harmonic_basis, step_size, kl_matrix):
    n_ma, n_pol, n_freq = sizes
    nfreq, _, nbase, ntime = visibility.shape
    local_modes, degrees = mode_gain.shape
    kept = kl_matrix.shape[0] // n_freq
    half = nfreq * nbase
    full = n_pol * half
    all_modes = local_modes * n_ma
    tchunks = 2 if ntime % 512 == 0 else 1
    table = spectral_tables(all_modes, ntime, ntime * n_ma)
    table = np.ascontiguousarray(table.T).reshape(tchunks, -1, 2 * all_modes)
    peers = n_ma * n_pol - 1
    hops, cores = max(n_freq - 1, 1), max(n_pol - 1, 1)
    dma = pltpu.SemaphoreType.DMA
    out_shape = (kept, local_modes, degrees)
    out = pl.pallas_call(
        functools.partial(kernel, sizes),
        out_shape=pltpu.VMEM(out_shape, jnp.bfloat16),
        in_specs=[pl.BlockSpec(memory_space=pl.ANY)] * 7,
        out_specs=pl.BlockSpec(memory_space=pltpu.VMEM),
        scratch_shapes=[
            pltpu.VMEM((2, nfreq, nbase, ntime), jnp.bfloat16),
            pltpu.VMEM(table.shape, jnp.bfloat16),
            pltpu.VMEM((n_freq, n_pol, nfreq, nbase, degrees), jnp.bfloat16),
            pltpu.VMEM((local_modes, degrees), jnp.float32),
            pltpu.VMEM(harmonic_basis.shape, jnp.bfloat16),
            pltpu.VMEM(harmonic_basis.shape[::-1], jnp.bfloat16),
            pltpu.VMEM((degrees, full), jnp.bfloat16),
            pltpu.SMEM(step_size.shape, jnp.float32),
            pltpu.VMEM(kl_matrix.shape, jnp.bfloat16),
            pltpu.VMEM((2, n_ma, local_modes, half), jnp.bfloat16),
            pltpu.VMEM((n_pol, n_ma, local_modes, half), jnp.bfloat16),
            pltpu.VMEM((hops, kept, local_modes, full), jnp.bfloat16),
            pltpu.VMEM((hops, kept, local_modes, full), jnp.bfloat16),
            dma((3 * tchunks + 5,)),
            dma((peers,)),
            dma((peers,)),
            dma((2, cores)),
            dma((2, hops)),
            dma((2, hops, cores)),
            dma((2, hops)),
        ],
        compiler_params=pltpu.CompilerParams(
            collective_id=0, has_side_effects=True, vmem_limit_bytes=56 * 2**20
        ),
    )(
        visibility,
        jnp.asarray(table),
        beam_rows,
        mode_gain,
        harmonic_basis,
        step_size,
        kl_matrix,
    )
    return out.transpose(1, 0, 2)[:, :, None, :]


def solution(mesh):
    sizes = (mesh.shape["ma"], mesh.shape["pol"], mesh.shape["freq"])
    placed = (
        P(("slab", "freq"), None, "pol", "ma"),
        P(("slab", "freq"), "pol", None),
        P("ma", None),
        P(),
        P(("slab", "freq")),
        P("slab", None),
    )
    return jax.shard_map(
        functools.partial(on_device, sizes),
        mesh=mesh,
        in_specs=placed,
        out_specs=P("ma", ("slab", "freq"), "pol", None),
        check_vma=False,
    )
```

```python
import functools

import jax
import jax.numpy as jnp
import ml_dtypes
import numpy as np
from jax import lax
from jax.experimental import pallas as pl
from jax.experimental.pallas import tpu as pltpu
from jax.sharding import PartitionSpec as P

ITERS = 2
MESH = pl.DeviceIdType.MESH


def spectral_tables(modes, local_time, total):
    phase = np.outer(np.arange(modes), np.arange(local_time)) % total
    angle = phase * (2.0 * np.pi / total)
    both = np.concatenate([np.cos(angle), np.sin(angle)], axis=0)
    return both.astype(np.float32).astype(ml_dtypes.bfloat16)


def dot(left, right):
    return jnp.dot(left, right, preferred_element_type=jnp.float32)


def kernel(
    sizes,
    vis_hbm,
    table_hbm,
    beam_hbm,
    gain_hbm,
    basis_hbm,
    step_hbm,
    kl_hbm,
    out_ref,
    vis_v,
    table_v,
    beam_v,
    gain_v,
    basis_v,
    basis_t,
    rows_t,
    step_s,
    kl_v,
    send_v,
    recv_v,
    ysend_v,
    yrecv_v,
    load_sem,
    send_sem,
    recv_sem,
    pol_sem,
    freq_sem,
    pass_sem,
    y_sem,
):
    n_ma, n_pol, n_freq = sizes
    a, p, fr = lax.axis_index("ma"), lax.axis_index("pol"), lax.axis_index("freq")
    _, nfreq, nbase, ntime = vis_v.shape
    local_modes, degrees = gain_v.shape
    all_modes = local_modes * n_ma
    half = nfreq * nbase
    full = n_pol * half
    kept = kl_v.shape[0] // n_freq
    pieces = table_v.shape[1]
    span = n_ma // pieces
    halves_of_ma = [lax.rem(a // span + 1 + piece, pieces) for piece in range(pieces)]

    barrier = pltpu.get_barrier_semaphore()

    def group_id(da, dp):
        return {"ma": lax.rem(a + da, n_ma), "pol": lax.rem(p + dp, n_pol)}

    def freq_id(df):
        return {"freq": lax.rem(fr + df, n_freq)}

    def remote(src, dst, send, recv, to):
        copy = pltpu.make_async_remote_copy(
            src_ref=src,
            dst_ref=dst,
            send_sem=send,
            recv_sem=recv,
            device_id=to,
            device_id_type=MESH,
        )
        copy.start()
        return copy

    for da, dp in [(da, dp) for da in range(n_ma) for dp in range(n_pol)][1:]:
        pl.semaphore_signal(barrier, inc=1, device_id=group_id(da, dp), device_id_type=MESH)
    for df in range(1, n_freq):
        pl.semaphore_signal(barrier, inc=1, device_id=freq_id(df), device_id_type=MESH)

    tchunks, tsize = table_v.shape[0], table_v.shape[2]
    vis_loads, table_loads = [], [[] for _ in range(pieces)]

    def load_table(piece, i):
        part = halves_of_ma[piece]
        sem = load_sem.at[tchunks * (2 + piece) + i]
        copy = pltpu.make_async_copy(table_hbm.at[i, part], table_v.at[i, part], sem)
        copy.start()
        table_loads[piece].append(copy)

    for i in range(tchunks):
        cols = pl.ds(i * tsize, tsize)
        group = [
            pltpu.make_async_copy(
                vis_hbm.at[:, part, :, cols], vis_v.at[part, :, :, cols], load_sem.at[2 * i + part]
            )
            for part in range(2)
        ]
        for c in group:
            c.start()
        vis_loads.append(group)
        load_table(0, i)
    for piece in range(1, pieces):
        for i in range(tchunks):
            load_table(piece, i)
    loads = [
        pltpu.make_async_copy(src, dst, load_sem.at[tchunks * (2 + pieces) + i])
        for i, (src, dst) in enumerate(
            [
                (step_hbm, step_s),
                (kl_hbm, kl_v),
                (basis_hbm, basis_v),
                (beam_hbm, beam_v.at[fr, p]),
                (gain_hbm, gain_v),
            ]
        )
    ]
    for c in loads:
        c.start()

    scale = float(ntime * n_ma) ** -0.5
    shape = (span, local_modes, half)
    copies = []
    for piece, part in enumerate(halves_of_ma):
        start = part * span
        total = None
        for i in range(tchunks):
            if piece == 0:
                for c in vis_loads[i]:
                    c.wait()
            table_loads[piece][i].wait()
            samples = vis_v[:, :, :, i * tsize : (i + 1) * tsize].reshape(2 * half, tsize)
            term = dot(samples, table_v[i, part])
            total = term if total is None else total + term
            if piece == 0 and i == 0:
                pl.semaphore_wait(barrier, n_ma * n_pol - 1 + n_freq - 1)
                mine = beam_v.at[fr, p]
                pol_copies = [
                    remote(beam_hbm, mine, pol_sem.at[0, d - 1], pol_sem.at[1, d - 1], group_id(0, d))
                    for d in range(1, n_pol)
                ]
                freq_copies = [
                    remote(beam_hbm, mine, freq_sem.at[0, d - 1], freq_sem.at[1, d - 1], freq_id(d))
                    for d in range(1, n_freq)
                ]
        total = total.T.reshape(span, 2, local_modes, 2 * half)
        real = total[:, 0, :, :half] + total[:, 1, :, half:]
        imag = total[:, 0, :, half:] - total[:, 1, :, :half]
        mode = lax.broadcasted_iota(jnp.int32, shape, 1) + local_modes * (
            start + lax.broadcasted_iota(jnp.int32, shape, 0)
        )
        turn = lax.rem(a * mode, n_ma)
        pc = jnp.full(shape, scale, jnp.float32)
        ps = jnp.zeros(shape, jnp.float32)
        for r in range(1, n_ma):
            angle = 2.0 * np.pi * r / n_ma
            pc = jnp.where(turn == r, float(scale * np.cos(angle)), pc)
            ps = jnp.where(turn == r, float(scale * np.sin(angle)), ps)
        send_v[0, pl.ds(start, span)] = (real * pc + imag * ps).astype(jnp.bfloat16)
        send_v[1, pl.ds(start, span)] = (imag * pc - real * ps).astype(jnp.bfloat16)

        for i in range(span):
            for dp in range(n_pol):
                if piece == pieces - 1 and (i, dp) == (0, 0):
                    continue
                to = {"ma": start + lax.rem(a + i, span), "pol": lax.rem(p + dp, n_pol)}
                src = send_v.at[to["pol"], to["ma"]]
                n = len(copies)
                copies.append(remote(src, recv_v.at[p, a], send_sem.at[n], recv_sem.at[n], to))
    recv_v[p, a] = send_v[p, a]

    for c in loads:
        c.wait()
    lane = lax.rem(lax.broadcasted_iota(jnp.int32, (local_modes, full), 1), half)
    own = [(lane >= f * nbase) & (lane < (f + 1) * nbase) for f in range(nfreq)]
    mode = lax.broadcasted_iota(jnp.int32, (local_modes, degrees), 0) + a * local_modes
    keep = lax.broadcasted_iota(jnp.int32, (local_modes, degrees), 1) >= mode
    kl = kl_v[...].astype(jnp.float32)
    kl_row = lax.broadcasted_iota(jnp.int32, kl.shape, 0)
    kl_col = lax.broadcasted_iota(jnp.int32, kl.shape, 1)

    def kl_weight(j, f):
        chosen = (kl_row == j) & (kl_col == fr * nfreq + f)
        return jnp.sum(jnp.where(chosen, kl, 0.0), axis=(0, 1), keepdims=True)

    def lane_weights(df):
        weights = []
        for j in range(kept):
            row = jnp.zeros((1, full), jnp.float32)
            for f in range(nfreq):
                value = kl_weight(lax.rem(fr + df, n_freq) * kept + j, f)
                row = jnp.where(own[f][:1], value, row)
            weights.append(row)
        return weights

    weights = [lane_weights(df) for df in range(n_freq)]
    steps = jnp.zeros((1, full), jnp.float32)
    for f in range(nfreq):
        steps = jnp.where(own[f][:1], step_s[f], steps)

    basis_t[...] = basis_v[...].T
    for copy in pol_copies:
        copy.wait_recv()
    rows_t[...] = beam_v[fr].reshape(full, degrees).T
    for copy in copies:
        copy.wait_recv()

    def spread(value):
        return jnp.concatenate(
            [jnp.where(own[f], value, 0.0) for f in range(nfreq)], axis=0
        ).astype(jnp.bfloat16)

    def gather(value):
        result = jnp.zeros((local_modes, full), jnp.float32)
        for f in range(nfreq):
            result = jnp.where(own[f], value[f * local_modes : (f + 1) * local_modes], result)
        return result

    def with_gain(value):
        value = value.reshape(-1, local_modes, degrees) * gain_v[...][None]
        return value.astype(jnp.bfloat16).reshape(-1, degrees)

    def masked(value):
        value = value.reshape(-1, local_modes, degrees)
        return jnp.where(keep[None], value, 0.0).astype(jnp.bfloat16).reshape(-1, degrees)

    def again(y):
        rows = beam_v[fr].reshape(full, degrees)
        coeffs = masked(dot(with_gain(dot(spread(y), rows)), basis_v[...]))
        return gather(dot(with_gain(dot(coeffs, basis_t[...])), rows_t[...]))

    halves = []
    for q in range(n_pol):
        summed = recv_v[q, 0].astype(jnp.float32)
        for s in range(1, n_ma):
            summed = summed + recv_v[q, s].astype(jnp.float32)
        halves.append(summed)
    z = steps * jnp.concatenate(halves, axis=1)
    y = z
    pass_copies = []
    for it in range(ITERS):
        y = y + z - steps * again(y)
        if it == 0:
            for d, copy in enumerate(freq_copies, 1):
                copy.wait_recv()
                slot = beam_v.at[lax.rem(fr + n_freq - d, n_freq), p]
                for dp in range(1, n_pol):
                    sems = (pass_sem.at[0, d - 1, dp - 1], pass_sem.at[1, d - 1, dp - 1])
                    pass_copies.append(remote(slot, slot, *sems, group_id(0, dp)))

    y_copies = []
    for d in range(1, n_freq):
        for j in range(kept):
            ysend_v[d - 1, j] = (y * weights[d][j]).astype(jnp.bfloat16)
        sems = (y_sem.at[0, d - 1], y_sem.at[1, d - 1])
        y_copies.append(remote(ysend_v.at[d - 1], yrecv_v.at[d - 1], *sems, freq_id(d)))

    left = jnp.concatenate([y * w for w in weights[0]], axis=0).astype(jnp.bfloat16)
    g = dot(left, beam_v[fr].reshape(full, degrees))
    for copy in pass_copies + y_copies:
        copy.wait_recv()
    for d in range(1, n_freq):
        left = yrecv_v[d - 1].reshape(kept * local_modes, full)
        source = lax.rem(fr + n_freq - d, n_freq)
        g = g + dot(left, beam_v[source].reshape(full, degrees))
    out_ref[...] = masked(dot(with_gain(g), basis_v[...])).reshape(out_ref.shape)
    for copy in copies + pol_copies + freq_copies + pass_copies + y_copies:
        copy.wait_send()


def on_device(sizes, visibility, beam_rows, mode_gain, harmonic_basis, step_size, kl_matrix):
    n_ma, n_pol, n_freq = sizes
    nfreq, _, nbase, ntime = visibility.shape
    local_modes, degrees = mode_gain.shape
    kept = kl_matrix.shape[0] // n_freq
    half = nfreq * nbase
    full = n_pol * half
    all_modes = local_modes * n_ma
    tchunks = 2 if ntime % 512 == 0 else 1
    pieces = 2 if n_ma % 2 == 0 else 1
    table = spectral_tables(all_modes, ntime, ntime * n_ma)
    table = table.reshape(2, pieces, n_ma // pieces, local_modes, tchunks, -1)
    table = np.ascontiguousarray(table.transpose(4, 1, 5, 2, 0, 3)).reshape(
        tchunks, pieces, ntime // tchunks, -1
    )
    peers = n_ma * n_pol - 1
    hops, cores = max(n_freq - 1, 1), max(n_pol - 1, 1)
    dma = pltpu.SemaphoreType.DMA
    out_shape = (kept, local_modes, degrees)
    out = pl.pallas_call(
        functools.partial(kernel, sizes),
        out_shape=pltpu.VMEM(out_shape, jnp.bfloat16),
        in_specs=[pl.BlockSpec(memory_space=pl.ANY)] * 7,
        out_specs=pl.BlockSpec(memory_space=pltpu.VMEM),
        scratch_shapes=[
            pltpu.VMEM((2, nfreq, nbase, ntime), jnp.bfloat16),
            pltpu.VMEM(table.shape, jnp.bfloat16),
            pltpu.VMEM((n_freq, n_pol, nfreq, nbase, degrees), jnp.bfloat16),
            pltpu.VMEM((local_modes, degrees), jnp.float32),
            pltpu.VMEM(harmonic_basis.shape, jnp.bfloat16),
            pltpu.VMEM(harmonic_basis.shape[::-1], jnp.bfloat16),
            pltpu.VMEM((degrees, full), jnp.bfloat16),
            pltpu.SMEM(step_size.shape, jnp.float32),
            pltpu.VMEM(kl_matrix.shape, jnp.bfloat16),
            pltpu.VMEM((2, n_ma, local_modes, half), jnp.bfloat16),
            pltpu.VMEM((n_pol, n_ma, local_modes, half), jnp.bfloat16),
            pltpu.VMEM((hops, kept, local_modes, full), jnp.bfloat16),
            pltpu.VMEM((hops, kept, local_modes, full), jnp.bfloat16),
            dma((tchunks * (2 + pieces) + 5,)),
            dma((peers,)),
            dma((peers,)),
            dma((2, cores)),
            dma((2, hops)),
            dma((2, hops, cores)),
            dma((2, hops)),
        ],
        compiler_params=pltpu.CompilerParams(
            collective_id=0, has_side_effects=True, vmem_limit_bytes=56 * 2**20
        ),
    )(
        visibility,
        jnp.asarray(table),
        beam_rows,
        mode_gain,
        harmonic_basis,
        step_size,
        kl_matrix,
    )
    return out.transpose(1, 0, 2)[:, :, None, :]


def solution(mesh):
    sizes = (mesh.shape["ma"], mesh.shape["pol"], mesh.shape["freq"])
    placed = (
        P(("slab", "freq"), None, "pol", "ma"),
        P(("slab", "freq"), "pol", None),
        P("ma", None),
        P(),
        P(("slab", "freq")),
        P("slab", None),
    )
    return jax.shard_map(
        functools.partial(on_device, sizes),
        mesh=mesh,
        in_specs=placed,
        out_specs=P("ma", ("slab", "freq"), "pol", None),
        check_vma=False,
    )
```

```python
import functools

import jax
import jax.numpy as jnp
import ml_dtypes
import numpy as np
from jax import lax
from jax.experimental import pallas as pl
from jax.experimental.pallas import tpu as pltpu
from jax.sharding import PartitionSpec as P

ITERS = 2
MESH = pl.DeviceIdType.MESH


def spectral_tables(modes, local_time, total):
    phase = np.outer(np.arange(modes), np.arange(local_time)) % total
    angle = phase * (2.0 * np.pi / total)
    both = np.concatenate([np.cos(angle), np.sin(angle)], axis=0)
    return both.astype(np.float32).astype(ml_dtypes.bfloat16)


def dot(left, right):
    return jnp.dot(left, right, preferred_element_type=jnp.float32)


def dot_t(left, right):
    last = (((1,), (1,)), ((), ()))
    return lax.dot_general(left, right, last, preferred_element_type=jnp.float32)


def kernel(
    sizes,
    vis_hbm,
    table_hbm,
    beam_hbm,
    gain_hbm,
    basis_hbm,
    step_hbm,
    kl_hbm,
    out_ref,
    vis_v,
    table_v,
    beam_v,
    gain_v,
    basis_v,
    step_s,
    kl_v,
    send_v,
    recv_v,
    ysend_v,
    yrecv_v,
    load_sem,
    send_sem,
    recv_sem,
    pol_sem,
    freq_sem,
    pass_sem,
    y_sem,
):
    n_ma, n_pol, n_freq = sizes
    a, p, fr = lax.axis_index("ma"), lax.axis_index("pol"), lax.axis_index("freq")
    _, nfreq, nbase, ntime = vis_v.shape
    local_modes, degrees = gain_v.shape
    all_modes = local_modes * n_ma
    half = nfreq * nbase
    full = n_pol * half
    kept = kl_v.shape[0] // n_freq
    pieces = table_v.shape[1]
    span = n_ma // pieces
    halves_of_ma = [lax.rem(a // span + 1 + piece, pieces) for piece in range(pieces)]

    barrier = pltpu.get_barrier_semaphore()

    def group_id(da, dp):
        return {"ma": lax.rem(a + da, n_ma), "pol": lax.rem(p + dp, n_pol)}

    def freq_id(df):
        return {"freq": lax.rem(fr + df, n_freq)}

    def remote(src, dst, send, recv, to):
        copy = pltpu.make_async_remote_copy(
            src_ref=src,
            dst_ref=dst,
            send_sem=send,
            recv_sem=recv,
            device_id=to,
            device_id_type=MESH,
        )
        copy.start()
        return copy

    for da, dp in [(da, dp) for da in range(n_ma) for dp in range(n_pol)][1:]:
        pl.semaphore_signal(barrier, inc=1, device_id=group_id(da, dp), device_id_type=MESH)
    for df in range(1, n_freq):
        pl.semaphore_signal(barrier, inc=1, device_id=freq_id(df), device_id_type=MESH)

    tchunks, tsize = table_v.shape[0], table_v.shape[2]
    vis_loads, table_loads = [], [[] for _ in range(pieces)]

    def load_table(piece, i):
        part = halves_of_ma[piece]
        sem = load_sem.at[tchunks * (2 + piece) + i]
        copy = pltpu.make_async_copy(table_hbm.at[i, part], table_v.at[i, part], sem)
        copy.start()
        table_loads[piece].append(copy)

    for i in range(tchunks):
        cols = pl.ds(i * tsize, tsize)
        group = [
            pltpu.make_async_copy(
                vis_hbm.at[:, part, :, cols], vis_v.at[part, :, :, cols], load_sem.at[2 * i + part]
            )
            for part in range(2)
        ]
        for c in group:
            c.start()
        vis_loads.append(group)
        load_table(0, i)
    for piece in range(1, pieces):
        for i in range(tchunks):
            load_table(piece, i)
    loads = [
        pltpu.make_async_copy(src, dst, load_sem.at[tchunks * (2 + pieces) + i])
        for i, (src, dst) in enumerate(
            [
                (step_hbm, step_s),
                (kl_hbm, kl_v),
                (basis_hbm, basis_v),
                (beam_hbm, beam_v.at[fr, p]),
                (gain_hbm, gain_v),
            ]
        )
    ]
    for c in loads:
        c.start()

    scale = float(ntime * n_ma) ** -0.5
    shape = (span, local_modes, half)
    copies = []
    for piece, part in enumerate(halves_of_ma):
        start = part * span
        total = None
        for i in range(tchunks):
            if piece == 0:
                for c in vis_loads[i]:
                    c.wait()
            table_loads[piece][i].wait()
            samples = vis_v[:, :, :, i * tsize : (i + 1) * tsize].reshape(2 * half, tsize)
            term = dot(samples, table_v[i, part])
            total = term if total is None else total + term
            if piece == 0 and i == 0:
                pl.semaphore_wait(barrier, n_ma * n_pol - 1 + n_freq - 1)
                mine = beam_v.at[fr, p]
                pol_copies = [
                    remote(beam_hbm, mine, pol_sem.at[0, d - 1], pol_sem.at[1, d - 1], group_id(0, d))
                    for d in range(1, n_pol)
                ]
                freq_copies = [
                    remote(beam_hbm, mine, freq_sem.at[0, d - 1], freq_sem.at[1, d - 1], freq_id(d))
                    for d in range(1, n_freq)
                ]
        total = total.T.reshape(span, 2, local_modes, 2 * half)
        real = total[:, 0, :, :half] + total[:, 1, :, half:]
        imag = total[:, 0, :, half:] - total[:, 1, :, :half]
        mode = lax.broadcasted_iota(jnp.int32, shape, 1) + local_modes * (
            start + lax.broadcasted_iota(jnp.int32, shape, 0)
        )
        turn = lax.rem(a * mode, n_ma)
        pc = jnp.full(shape, scale, jnp.float32)
        ps = jnp.zeros(shape, jnp.float32)
        for r in range(1, n_ma):
            angle = 2.0 * np.pi * r / n_ma
            pc = jnp.where(turn == r, float(scale * np.cos(angle)), pc)
            ps = jnp.where(turn == r, float(scale * np.sin(angle)), ps)
        send_v[0, pl.ds(start, span)] = (real * pc + imag * ps).astype(jnp.bfloat16)
        send_v[1, pl.ds(start, span)] = (imag * pc - real * ps).astype(jnp.bfloat16)

        for i in range(span):
            for dp in range(n_pol):
                if piece == pieces - 1 and (i, dp) == (0, 0):
                    continue
                to = {"ma": start + lax.rem(a + i, span), "pol": lax.rem(p + dp, n_pol)}
                src = send_v.at[to["pol"], to["ma"]]
                n = len(copies)
                copies.append(remote(src, recv_v.at[p, a], send_sem.at[n], recv_sem.at[n], to))
    recv_v[p, a] = send_v[p, a]

    for c in loads:
        c.wait()
    lane = lax.rem(lax.broadcasted_iota(jnp.int32, (local_modes, full), 1), half)
    own = [(lane >= f * nbase) & (lane < (f + 1) * nbase) for f in range(nfreq)]
    mode = lax.broadcasted_iota(jnp.int32, (local_modes, degrees), 0) + a * local_modes
    keep = lax.broadcasted_iota(jnp.int32, (local_modes, degrees), 1) >= mode
    kl = kl_v[...].astype(jnp.float32)
    kl_row = lax.broadcasted_iota(jnp.int32, kl.shape, 0)
    kl_col = lax.broadcasted_iota(jnp.int32, kl.shape, 1)

    def kl_weight(j, f):
        chosen = (kl_row == j) & (kl_col == fr * nfreq + f)
        return jnp.sum(jnp.where(chosen, kl, 0.0), axis=(0, 1), keepdims=True)

    def lane_weights(df):
        weights = []
        for j in range(kept):
            row = jnp.zeros((1, full), jnp.float32)
            for f in range(nfreq):
                value = kl_weight(lax.rem(fr + df, n_freq) * kept + j, f)
                row = jnp.where(own[f][:1], value, row)
            weights.append(row)
        return weights

    weights = [lane_weights(df) for df in range(n_freq)]
    steps = jnp.zeros((1, full), jnp.float32)
    for f in range(nfreq):
        steps = jnp.where(own[f][:1], step_s[f], steps)

    for copy in pol_copies + copies:
        copy.wait_recv()

    def spread(value):
        return jnp.concatenate(
            [jnp.where(own[f], value, 0.0) for f in range(nfreq)], axis=0
        ).astype(jnp.bfloat16)

    def gather(value):
        result = jnp.zeros((local_modes, full), jnp.float32)
        for f in range(nfreq):
            result = jnp.where(own[f], value[f * local_modes : (f + 1) * local_modes], result)
        return result

    def with_gain(value):
        value = value.reshape(-1, local_modes, degrees) * gain_v[...][None]
        return value.astype(jnp.bfloat16).reshape(-1, degrees)

    def masked(value):
        value = value.reshape(-1, local_modes, degrees)
        return jnp.where(keep[None], value, 0.0).astype(jnp.bfloat16).reshape(-1, degrees)

    def again(y):
        rows = beam_v[fr].reshape(full, degrees)
        coeffs = masked(dot(with_gain(dot(spread(y), rows)), basis_v[...]))
        return gather(dot_t(with_gain(dot_t(coeffs, basis_v[...])), rows))

    halves = []
    for q in range(n_pol):
        summed = recv_v[q, 0].astype(jnp.float32)
        for s in range(1, n_ma):
            summed = summed + recv_v[q, s].astype(jnp.float32)
        halves.append(summed)
    z = steps * jnp.concatenate(halves, axis=1)
    y = z
    pass_copies = []
    for it in range(ITERS):
        y = y + z - steps * again(y)
        if it == 0:
            for d, copy in enumerate(freq_copies, 1):
                copy.wait_recv()
                slot = beam_v.at[lax.rem(fr + n_freq - d, n_freq), p]
                for dp in range(1, n_pol):
                    sems = (pass_sem.at[0, d - 1, dp - 1], pass_sem.at[1, d - 1, dp - 1])
                    pass_copies.append(remote(slot, slot, *sems, group_id(0, dp)))

    y_copies = []
    for d in range(1, n_freq):
        for j in range(kept):
            ysend_v[d - 1, j] = (y * weights[d][j]).astype(jnp.bfloat16)
        sems = (y_sem.at[0, d - 1], y_sem.at[1, d - 1])
        y_copies.append(remote(ysend_v.at[d - 1], yrecv_v.at[d - 1], *sems, freq_id(d)))

    left = jnp.concatenate([y * w for w in weights[0]], axis=0).astype(jnp.bfloat16)
    g = dot(left, beam_v[fr].reshape(full, degrees))
    for copy in pass_copies + y_copies:
        copy.wait_recv()
    for d in range(1, n_freq):
        left = yrecv_v[d - 1].reshape(kept * local_modes, full)
        source = lax.rem(fr + n_freq - d, n_freq)
        g = g + dot(left, beam_v[source].reshape(full, degrees))
    out_ref[...] = masked(dot(with_gain(g), basis_v[...])).reshape(out_ref.shape)
    for copy in copies + pol_copies + freq_copies + pass_copies + y_copies:
        copy.wait_send()


def on_device(sizes, visibility, beam_rows, mode_gain, harmonic_basis, step_size, kl_matrix):
    n_ma, n_pol, n_freq = sizes
    nfreq, _, nbase, ntime = visibility.shape
    local_modes, degrees = mode_gain.shape
    kept = kl_matrix.shape[0] // n_freq
    half = nfreq * nbase
    full = n_pol * half
    all_modes = local_modes * n_ma
    tchunks = 2 if ntime % 512 == 0 else 1
    pieces = 2 if n_ma % 2 == 0 else 1
    table = spectral_tables(all_modes, ntime, ntime * n_ma)
    table = table.reshape(2, pieces, n_ma // pieces, local_modes, tchunks, -1)
    table = np.ascontiguousarray(table.transpose(4, 1, 5, 2, 0, 3)).reshape(
        tchunks, pieces, ntime // tchunks, -1
    )
    peers = n_ma * n_pol - 1
    hops, cores = max(n_freq - 1, 1), max(n_pol - 1, 1)
    dma = pltpu.SemaphoreType.DMA
    out_shape = (kept, local_modes, degrees)
    out = pl.pallas_call(
        functools.partial(kernel, sizes),
        out_shape=pltpu.VMEM(out_shape, jnp.bfloat16),
        in_specs=[pl.BlockSpec(memory_space=pl.ANY)] * 7,
        out_specs=pl.BlockSpec(memory_space=pltpu.VMEM),
        scratch_shapes=[
            pltpu.VMEM((2, nfreq, nbase, ntime), jnp.bfloat16),
            pltpu.VMEM(table.shape, jnp.bfloat16),
            pltpu.VMEM((n_freq, n_pol, nfreq, nbase, degrees), jnp.bfloat16),
            pltpu.VMEM((local_modes, degrees), jnp.float32),
            pltpu.VMEM(harmonic_basis.shape, jnp.bfloat16),
            pltpu.SMEM(step_size.shape, jnp.float32),
            pltpu.VMEM(kl_matrix.shape, jnp.bfloat16),
            pltpu.VMEM((2, n_ma, local_modes, half), jnp.bfloat16),
            pltpu.VMEM((n_pol, n_ma, local_modes, half), jnp.bfloat16),
            pltpu.VMEM((hops, kept, local_modes, full), jnp.bfloat16),
            pltpu.VMEM((hops, kept, local_modes, full), jnp.bfloat16),
            dma((tchunks * (2 + pieces) + 5,)),
            dma((peers,)),
            dma((peers,)),
            dma((2, cores)),
            dma((2, hops)),
            dma((2, hops, cores)),
            dma((2, hops)),
        ],
        compiler_params=pltpu.CompilerParams(
            collective_id=0, has_side_effects=True, vmem_limit_bytes=56 * 2**20
        ),
    )(
        visibility,
        jnp.asarray(table),
        beam_rows,
        mode_gain,
        harmonic_basis,
        step_size,
        kl_matrix,
    )
    return out.transpose(1, 0, 2)[:, :, None, :]


def solution(mesh):
    sizes = (mesh.shape["ma"], mesh.shape["pol"], mesh.shape["freq"])
    placed = (
        P(("slab", "freq"), None, "pol", "ma"),
        P(("slab", "freq"), "pol", None),
        P("ma", None),
        P(),
        P(("slab", "freq")),
        P("slab", None),
    )
    return jax.shard_map(
        functools.partial(on_device, sizes),
        mesh=mesh,
        in_specs=placed,
        out_specs=P("ma", ("slab", "freq"), "pol", None),
        check_vma=False,
    )
```

```python
import functools

import jax
import jax.numpy as jnp
import ml_dtypes
import numpy as np
from jax import lax
from jax.experimental import pallas as pl
from jax.experimental.pallas import tpu as pltpu
from jax.sharding import PartitionSpec as P

ITERS = 2
MESH = pl.DeviceIdType.MESH


def spectral_tables(modes, local_time, total):
    phase = np.outer(np.arange(modes), np.arange(local_time)) % total
    angle = phase * (2.0 * np.pi / total)
    both = np.concatenate([np.cos(angle), np.sin(angle)], axis=0)
    return both.astype(np.float32).astype(ml_dtypes.bfloat16)


def dot(left, right):
    return jnp.dot(left, right, preferred_element_type=jnp.float32)


def kernel(
    sizes,
    vis_hbm,
    table_hbm,
    beam_hbm,
    gain_hbm,
    basis_hbm,
    step_hbm,
    kl_hbm,
    out_ref,
    vis_v,
    table_v,
    beam_v,
    gain_v,
    basis_v,
    basis_t,
    rows_t,
    step_s,
    kl_v,
    send_v,
    recv_v,
    ysend_v,
    yrecv_v,
    load_sem,
    send_sem,
    recv_sem,
    pol_sem,
    freq_sem,
    pass_sem,
    y_sem,
):
    n_ma, n_pol, n_freq = sizes
    a, p, fr = lax.axis_index("ma"), lax.axis_index("pol"), lax.axis_index("freq")
    _, nfreq, nbase, ntime = vis_v.shape
    local_modes, degrees = gain_v.shape
    all_modes = local_modes * n_ma
    half = nfreq * nbase
    full = n_pol * half
    kept = kl_v.shape[0] // n_freq
    peers = [(da, dp) for da in range(n_ma) for dp in range(n_pol) if (da, dp) != (0, 0)]
    peers.sort(key=lambda o: (abs(o[0] - n_ma // 2), o[1]))

    barrier = pltpu.get_barrier_semaphore()

    def group_id(da, dp):
        return {"ma": lax.rem(a + da, n_ma), "pol": lax.rem(p + dp, n_pol)}

    def freq_id(df):
        return {"freq": lax.rem(fr + df, n_freq)}

    def remote(src, dst, send, recv, to):
        copy = pltpu.make_async_remote_copy(
            src_ref=src,
            dst_ref=dst,
            send_sem=send,
            recv_sem=recv,
            device_id=to,
            device_id_type=MESH,
        )
        copy.start()
        return copy

    for da, dp in peers:
        pl.semaphore_signal(barrier, inc=1, device_id=group_id(da, dp), device_id_type=MESH)
    for df in range(1, n_freq):
        pl.semaphore_signal(barrier, inc=1, device_id=freq_id(df), device_id_type=MESH)

    tchunks = table_v.shape[0]
    tsize = ntime // tchunks
    spectral = []
    for i in range(tchunks):
        cols = pl.ds(i * tsize, tsize)
        group = [
            pltpu.make_async_copy(
                vis_hbm.at[:, part, :, cols], vis_v.at[part, :, :, cols], load_sem.at[3 * i + part]
            )
            for part in range(2)
        ]
        group.append(pltpu.make_async_copy(table_hbm.at[i], table_v.at[i], load_sem.at[3 * i + 2]))
        for c in group:
            c.start()
        spectral.append(group)
    loads = [
        pltpu.make_async_copy(src, dst, load_sem.at[3 * tchunks + i])
        for i, (src, dst) in enumerate(
            [
                (step_hbm, step_s),
                (kl_hbm, kl_v),
                (basis_hbm, basis_v),
                (beam_hbm, beam_v.at[fr, p]),
                (gain_hbm, gain_v),
            ]
        )
    ]
    for c in loads:
        c.start()

    total = None
    for i in range(tchunks):
        for c in spectral[i]:
            c.wait()
        samples = vis_v[:, :, :, i * tsize : (i + 1) * tsize].reshape(2 * half, tsize)
        term = dot(samples, table_v[i])
        total = term if total is None else total + term
        if i == 0:
            pl.semaphore_wait(barrier, len(peers) + n_freq - 1)
            mine = beam_v.at[fr, p]
            pol_copies = [
                remote(beam_hbm, mine, pol_sem.at[0, d - 1], pol_sem.at[1, d - 1], group_id(0, d))
                for d in range(1, n_pol)
            ]
            freq_copies = [
                remote(beam_hbm, mine, freq_sem.at[0, d - 1], freq_sem.at[1, d - 1], freq_id(d))
                for d in range(1, n_freq)
            ]
    total = total.T
    cosine, sine = total[:all_modes], total[all_modes:]
    real = cosine[:, :half] + sine[:, half:]
    imag = cosine[:, half:] - sine[:, :half]
    turn = lax.rem(a * lax.broadcasted_iota(jnp.int32, (all_modes, half), 0), n_ma)
    scale = float(ntime * n_ma) ** -0.5
    pc = jnp.full((all_modes, half), scale, jnp.float32)
    ps = jnp.zeros((all_modes, half), jnp.float32)
    for r in range(1, n_ma):
        angle = 2.0 * np.pi * r / n_ma
        pc = jnp.where(turn == r, float(scale * np.cos(angle)), pc)
        ps = jnp.where(turn == r, float(scale * np.sin(angle)), ps)
    block = (n_ma, local_modes, half)
    send_v[0] = (real * pc + imag * ps).astype(jnp.bfloat16).reshape(block)
    send_v[1] = (imag * pc - real * ps).astype(jnp.bfloat16).reshape(block)

    copies = []
    for i, (da, dp) in enumerate(peers):
        to = group_id(da, dp)
        src = send_v.at[to["pol"], to["ma"]]
        copies.append(remote(src, recv_v.at[p, a], send_sem.at[i], recv_sem.at[i], to))
    recv_v[p, a] = send_v[p, a]

    for c in loads:
        c.wait()
    lane = lax.rem(lax.broadcasted_iota(jnp.int32, (local_modes, full), 1), half)
    own = [(lane >= f * nbase) & (lane < (f + 1) * nbase) for f in range(nfreq)]
    mode = lax.broadcasted_iota(jnp.int32, (local_modes, degrees), 0) + a * local_modes
    keep = lax.broadcasted_iota(jnp.int32, (local_modes, degrees), 1) >= mode
    kl = kl_v[...].astype(jnp.float32)
    kl_row = lax.broadcasted_iota(jnp.int32, kl.shape, 0)
    kl_col = lax.broadcasted_iota(jnp.int32, kl.shape, 1)

    def kl_weight(j, f):
        chosen = (kl_row == j) & (kl_col == fr * nfreq + f)
        return jnp.sum(jnp.where(chosen, kl, 0.0), axis=(0, 1), keepdims=True)

    def lane_weights(df):
        weights = []
        for j in range(kept):
            row = jnp.zeros((1, full), jnp.float32)
            for f in range(nfreq):
                value = kl_weight(lax.rem(fr + df, n_freq) * kept + j, f)
                row = jnp.where(own[f][:1], value, row)
            weights.append(row)
        return weights

    weights = [lane_weights(df) for df in range(n_freq)]
    steps = jnp.zeros((1, full), jnp.float32)
    for f in range(nfreq):
        steps = jnp.where(own[f][:1], step_s[f], steps)

    basis_t[...] = basis_v[...].T
    for copy in pol_copies:
        copy.wait_recv()
    rows_t[...] = beam_v[fr].reshape(full, degrees).T
    for copy in copies:
        copy.wait_recv()

    def with_gain(value):
        value = value.reshape(-1, local_modes, degrees) * gain_v[...][None]
        return value.astype(jnp.bfloat16).reshape(-1, degrees)

    def masked(value):
        value = value.reshape(-1, local_modes, degrees)
        return jnp.where(keep[None], value, 0.0).astype(jnp.bfloat16).reshape(-1, degrees)

    cut = (nfreq + 1) // 2
    chains = [fs for fs in (range(cut), range(cut, nfreq)) if len(fs) > 0]

    def again(y):
        rows = beam_v[fr].reshape(full, degrees)
        parts = [
            jnp.concatenate([jnp.where(own[f], y, 0.0) for f in fs], axis=0).astype(jnp.bfloat16)
            for fs in chains
        ]
        parts = [with_gain(dot(part, rows)) for part in parts]
        parts = [masked(dot(part, basis_v[...])) for part in parts]
        parts = [with_gain(dot(part, basis_t[...])) for part in parts]
        parts = [dot(part, rows_t[...]) for part in parts]
        result = jnp.zeros((local_modes, full), jnp.float32)
        for fs, part in zip(chains, parts):
            for i, f in enumerate(fs):
                result = jnp.where(own[f], part[i * local_modes : (i + 1) * local_modes], result)
        return result

    halves = []
    for q in range(n_pol):
        summed = recv_v[q, 0].astype(jnp.float32)
        for s in range(1, n_ma):
            summed = summed + recv_v[q, s].astype(jnp.float32)
        halves.append(summed)
    z = steps * jnp.concatenate(halves, axis=1)
    y = z
    pass_copies = []
    for it in range(ITERS):
        y = y + z - steps * again(y)
        if it == 0:
            for d, copy in enumerate(freq_copies, 1):
                copy.wait_recv()
                slot = beam_v.at[lax.rem(fr + n_freq - d, n_freq), p]
                for dp in range(1, n_pol):
                    sems = (pass_sem.at[0, d - 1, dp - 1], pass_sem.at[1, d - 1, dp - 1])
                    pass_copies.append(remote(slot, slot, *sems, group_id(0, dp)))

    y_copies = []
    for d in range(1, n_freq):
        for j in range(kept):
            ysend_v[d - 1, j] = (y * weights[d][j]).astype(jnp.bfloat16)
        sems = (y_sem.at[0, d - 1], y_sem.at[1, d - 1])
        y_copies.append(remote(ysend_v.at[d - 1], yrecv_v.at[d - 1], *sems, freq_id(d)))

    left = jnp.concatenate([y * w for w in weights[0]], axis=0).astype(jnp.bfloat16)
    g = dot(left, beam_v[fr].reshape(full, degrees))
    for copy in pass_copies + y_copies:
        copy.wait_recv()
    for d in range(1, n_freq):
        left = yrecv_v[d - 1].reshape(kept * local_modes, full)
        source = lax.rem(fr + n_freq - d, n_freq)
        g = g + dot(left, beam_v[source].reshape(full, degrees))
    out_ref[...] = masked(dot(with_gain(g), basis_v[...])).reshape(out_ref.shape)
    for copy in copies + pol_copies + freq_copies + pass_copies + y_copies:
        copy.wait_send()


def on_device(sizes, visibility, beam_rows, mode_gain, harmonic_basis, step_size, kl_matrix):
    n_ma, n_pol, n_freq = sizes
    nfreq, _, nbase, ntime = visibility.shape
    local_modes, degrees = mode_gain.shape
    kept = kl_matrix.shape[0] // n_freq
    half = nfreq * nbase
    full = n_pol * half
    all_modes = local_modes * n_ma
    tchunks = 2 if ntime % 512 == 0 else 1
    table = spectral_tables(all_modes, ntime, ntime * n_ma)
    table = np.ascontiguousarray(table.T).reshape(tchunks, -1, 2 * all_modes)
    peers = n_ma * n_pol - 1
    hops, cores = max(n_freq - 1, 1), max(n_pol - 1, 1)
    dma = pltpu.SemaphoreType.DMA
    out_shape = (kept, local_modes, degrees)
    out = pl.pallas_call(
        functools.partial(kernel, sizes),
        out_shape=pltpu.VMEM(out_shape, jnp.bfloat16),
        in_specs=[pl.BlockSpec(memory_space=pl.ANY)] * 7,
        out_specs=pl.BlockSpec(memory_space=pltpu.VMEM),
        scratch_shapes=[
            pltpu.VMEM((2, nfreq, nbase, ntime), jnp.bfloat16),
            pltpu.VMEM(table.shape, jnp.bfloat16),
            pltpu.VMEM((n_freq, n_pol, nfreq, nbase, degrees), jnp.bfloat16),
            pltpu.VMEM((local_modes, degrees), jnp.float32),
            pltpu.VMEM(harmonic_basis.shape, jnp.bfloat16),
            pltpu.VMEM(harmonic_basis.shape[::-1], jnp.bfloat16),
            pltpu.VMEM((degrees, full), jnp.bfloat16),
            pltpu.SMEM(step_size.shape, jnp.float32),
            pltpu.VMEM(kl_matrix.shape, jnp.bfloat16),
            pltpu.VMEM((2, n_ma, local_modes, half), jnp.bfloat16),
            pltpu.VMEM((n_pol, n_ma, local_modes, half), jnp.bfloat16),
            pltpu.VMEM((hops, kept, local_modes, full), jnp.bfloat16),
            pltpu.VMEM((hops, kept, local_modes, full), jnp.bfloat16),
            dma((3 * tchunks + 5,)),
            dma((peers,)),
            dma((peers,)),
            dma((2, cores)),
            dma((2, hops)),
            dma((2, hops, cores)),
            dma((2, hops)),
        ],
        compiler_params=pltpu.CompilerParams(
            collective_id=0, has_side_effects=True, vmem_limit_bytes=56 * 2**20
        ),
    )(
        visibility,
        jnp.asarray(table),
        beam_rows,
        mode_gain,
        harmonic_basis,
        step_size,
        kl_matrix,
    )
    return out.transpose(1, 0, 2)[:, :, None, :]


def solution(mesh):
    sizes = (mesh.shape["ma"], mesh.shape["pol"], mesh.shape["freq"])
    placed = (
        P(("slab", "freq"), None, "pol", "ma"),
        P(("slab", "freq"), "pol", None),
        P("ma", None),
        P(),
        P(("slab", "freq")),
        P("slab", None),
    )
    return jax.shard_map(
        functools.partial(on_device, sizes),
        mesh=mesh,
        in_specs=placed,
        out_specs=P("ma", ("slab", "freq"), "pol", None),
        check_vma=False,
    )
```
